512 devices in a mesh: group: 16 (over x, y_lo, core), expert: 32 (over y_hi, z).
Axes of the slice: x: 4, y: 8 (y_hi: 4, y_lo: 2; y = y_hi * 2 + y_lo), z: 8, core: 2. Of those that a mesh axis runs over, the one named last changes fastest.
Arguments:
- tokens: bfloat16 [16, 4096, 4096], P('group', 'expert'), may hold values from -6 to 6
- grad_out: bfloat16 [16, 4096, 4096], P('group', 'expert'), may hold values from -1.5 to 1.5
- gate_w: bfloat16 [4096, 4096], P('group', 'expert'), may hold values from -0.09375 to 0.09375
- up_w: bfloat16 [4096, 4096], P('group', 'expert'), may hold values from -0.09375 to 0.09375
- down_w: bfloat16 [4096, 4096], P('group', 'expert'), may hold values from -0.09375 to 0.09375
- take_count: int32 [16, 32], P('group', 'expert'), may hold values from 0 to 6, as said below
- take_rows: int32 [16, 32, 6], P('group', 'expert'), may hold values from 0 to 127, as said below
Outputs:
- grad_tokens: bfloat16 [16, 4096, 4096], P('group', 'expert')
- grad_gate: bfloat16 [4096, 4096], P('group', 'expert')
- grad_up: bfloat16 [4096, 4096], P('group', 'expert')
- grad_down: bfloat16 [4096, 4096], P('group', 'expert')
The draws below stay inside these ranges and needn't reach their ends.
Inputs may be any that keep to these rules, and one draw needn't show every extreme that they name: `take_count`: in every group the expert takes 6 rows from some index. `take_rows`: row numbers are distinct within each (g, o); slots at or past take_count are ignored.
All inputs are finite; a program needn't handle non-finite values.
Results may differ from the reference program's by a relative error of at most 0.0065.
Values may be sent and summed in bfloat16 or wider, within the bound.
A program may use at most 64 MiB of HBM per device.

```python
import jax
import jax.numpy as jnp
from jax import lax

D = 4096
HID = 4096
SLOT = 6
TOK_DEV = 128
TOK_GROUP = 4096
N_GROUP = 16
N_EXPERT = 32


def draw_take_count(key, part):
    key_speed, key_count, key_full = jax.random.split(key, 3)
    shape_all = (N_GROUP, N_EXPERT)
    speeds = jax.random.randint(key_speed, shape_all, 0, 3)
    floor_count = SLOT * speeds // 4
    drawn = jax.random.randint(key_count, shape_all, 0, SLOT + 1)
    counts = jnp.maximum(drawn, floor_count)
    filled = jax.random.randint(key_full, (N_GROUP, 1), 0, N_EXPERT)
    select = lax.broadcasted_iota(jnp.int32, shape_all, 1) == filled
    return jnp.where(select, SLOT, counts).astype(jnp.int32)


def draw_take_rows(key, part):
    shape_all = (N_GROUP, N_EXPERT, TOK_DEV)
    scores = jax.random.randint(key, shape_all, 0, 2 ** 17)
    column = lax.broadcasted_iota(jnp.int32, shape_all, 2)
    scores = scores * TOK_DEV + column
    corners = (lax.broadcasted_iota(jnp.int32, shape_all, 0) == 0) & (lax.broadcasted_iota(jnp.int32, shape_all, 1) == 0)
    scores = jnp.where(corners & (column == TOK_DEV - 1), 2 ** 30, scores)
    scores = jnp.where(corners & (column == 0), 2 ** 30 - 1, scores)
    chosen = lax.top_k(scores, SLOT)[1]
    return chosen.astype(jnp.int32)


def spiked(values, stream_key, source, target, blocks, factor):
    def block_of(axis_at):
        return (jnp.arange(values.shape[axis_at]) // (values.shape[axis_at] // blocks)).reshape((-1,) + (1,) * (values.ndim - 1 - axis_at))

    first = jax.random.permutation(stream_key, blocks)[block_of(target)]
    other_side = (block_of(target) + blocks // 2) % blocks
    return jnp.where((block_of(source) == first) | (block_of(source) == other_side), factor * values, values)


def block_scale(stream_key, extent, cuts, least, largest):
    factor_of = 1.0
    for dim, parts in cuts:
        steps = jax.random.uniform(jax.random.fold_in(jax.random.fold_in(stream_key, 6), dim), (parts,), jnp.float32, least / len(cuts), largest / len(cuts))
        factor_of = factor_of * jnp.repeat(jnp.exp(steps), extent[dim] // parts).reshape((-1,) + (1,) * (len(extent) - 1 - dim))
    return factor_of


def bell_draw(rng, extent, scale, most, shards=(), kind=jnp.bfloat16):
    level = block_scale(rng, extent, shards, -0.22, 0.18) if shards else 1.0
    values = jax.random.normal(rng, extent, jnp.float32) * scale * level
    return jnp.minimum(jnp.maximum(values, -most), most).astype(kind)


def heavy_noise(key, shape, deviation, reach, cuts, heavy, kind=jnp.bfloat16):
    array = deviation * jax.random.normal(key, shape, jnp.float32)
    if cuts:
        array = array * block_scale(key, shape, cuts, -0.22, 0.18)
    return jnp.clip(spiked(array, jax.random.fold_in(key, 3), *heavy), -reach, reach).astype(kind)


def setup_inputs(seed: int = 0) -> dict:
    key_of = jax.random.split(jax.random.key(seed), 8)
    return {
        "tokens": heavy_noise(key_of[0], (N_GROUP, TOK_GROUP, D), 1.0, 6.0, ((0, 16), (1, 32)), (0, 2, 16, 2.0)),
        "grad_out": heavy_noise(key_of[1], (N_GROUP, TOK_GROUP, D), 0.25, 1.5, ((0, 16), (1, 32)), (0, 2, 16, 2.0)),
        "gate_w": bell_draw(key_of[2], (D, HID), D ** -0.5, 0.09375, ((0, 16), (1, 32))),
        "up_w": bell_draw(key_of[3], (D, HID), D ** -0.5, 0.09375, ((0, 16), (1, 32))),
        "down_w": bell_draw(key_of[4], (D, HID), HID ** -0.5, 0.09375, ((0, 16), (1, 32))),
        "take_count": draw_take_count(jax.random.fold_in(key_of[7], 71), 0),
        "take_rows": draw_take_rows(jax.random.fold_in(key_of[7], 71), 0),
    }


def reference(tokens, grad_out, gate_w, up_w, down_w, take_count, take_rows):
    x_blocks = tokens.reshape(N_GROUP, N_EXPERT, TOK_DEV, D)
    dy_blocks = grad_out.reshape(N_GROUP, N_EXPERT, TOK_DEV, D)
    slot_index = jnp.arange(SLOT, dtype=jnp.int32)
    owner_index = jnp.arange(N_EXPERT, dtype=jnp.int32)
    w_gate_up = jnp.concatenate([gate_w, up_w], axis=1)

    def group_step(totals, inputs):
        x_group, dy_group, counts, picked = inputs
        live_slot = (slot_index[None, :] < counts[:, None])[:, :, None]
        nothing = jnp.zeros((), x_group.dtype)
        x_rows = jnp.where(live_slot, x_group[owner_index[:, None], picked], nothing).reshape(-1, D)
        dy_rows = jnp.where(live_slot, dy_group[owner_index[:, None], picked], nothing).reshape(-1, D)
        gate_up = jnp.dot(x_rows, w_gate_up, preferred_element_type=jnp.float32)
        grad_hidden = jnp.dot(dy_rows, down_w, preferred_element_type=jnp.float32)
        gate_pre = gate_up[:, :HID]
        up_pre = gate_up[:, HID:]
        sigmoid_g = jax.nn.sigmoid(gate_pre)
        gate_act = gate_pre * sigmoid_g
        hidden_act = (gate_act * up_pre).astype(jnp.bfloat16)
        d_up = (grad_hidden * gate_act).astype(jnp.bfloat16)
        d_gate = (grad_hidden * up_pre * sigmoid_g * (1.0 + gate_pre * (1.0 - sigmoid_g))).astype(jnp.bfloat16)
        joined = jnp.concatenate([d_gate, d_up], axis=1)
        grad_rows = jnp.dot(joined, w_gate_up.T, preferred_element_type=jnp.float32)
        owners = jnp.broadcast_to(owner_index[:, None], picked.shape)
        summed = jnp.zeros((N_EXPERT, TOK_DEV, D), jnp.float32)
        summed = summed.at[owners, picked].add(grad_rows.reshape(N_EXPERT, SLOT, D))
        first = totals[0] + jnp.dot(x_rows.T, joined, preferred_element_type=jnp.float32)
        second = totals[1] + jnp.dot(dy_rows.T, hidden_act, preferred_element_type=jnp.float32)
        return (first, second), summed.astype(jnp.bfloat16).reshape(TOK_GROUP, D)

    init = (jnp.zeros((D, 2 * HID), jnp.float32), jnp.zeros((D, HID), jnp.float32))
    totals, grad_tokens = lax.scan(group_step, init, (x_blocks, dy_blocks, take_count, take_rows))
    inverse = 1.0 / N_GROUP
    grad_gate = (totals[0][:, :HID] * inverse).astype(jnp.bfloat16)
    grad_up = (totals[0][:, HID:] * inverse).astype(jnp.bfloat16)
    grad_down = (totals[1] * inverse).astype(jnp.bfloat16)
    return grad_tokens, grad_gate, grad_up, grad_down
```

```python
import jax
import jax.numpy as jnp
import numpy as np
from jax import lax
from jax.experimental import pallas as pl
from jax.experimental.pallas import tpu as pltpu
from jax.sharding import PartitionSpec as P

BF = jnp.bfloat16
F32 = jnp.float32
SLOT = 6
NX, NYH, NZ = 4, 4, 8
TOK = 128
D = 4096
HD = 128
DB = 256
Q = 8
QW = D // Q
ROWS = NYH * SLOT
CH = 4
CW = QW // CH
MESH = pl.DeviceIdType.MESH


def mod(a, n):
    return lax.rem(a + n, n)


def gather_perm():
    n = NYH * Q * 2 * SLOT
    m = np.zeros((n, n), np.float32)
    for u in range(NYH):
        for q in range(Q):
            for t in range(2):
                for s in range(SLOT):
                    m[((q * 2 + t) * NYH + u) * SLOT + s, ((u * Q + q) * 2 + t) * SLOT + s] = 1
    return m


def scatter_perm():
    n = NYH * Q * SLOT
    m = np.zeros((n, n), np.float32)
    for u in range(NYH):
        for q in range(Q):
            for s in range(SLOT):
                m[(u * Q + q) * SLOT + s, (q * NYH + u) * SLOT + s] = 1
    return m


def kernel(
    tok_hbm, dy_hbm, gw_ref, uw_ref, dw_ref, cnt_ref, row_ref, gp_ref, sp_ref,
    gt_ref, gg_ref, gu_ref, gd_ref,
    td, Z, R, W, PRE, A, AT, J, PP, Y0, YR, ZS, ZR, SS, ES, ER, XS, XR, LS, LR,
    in_sem, zss, zrs, yss, yrs, wl, wxs, wxr, wcs, wcr, rzs, rzr, rys, ryr, ecs, ecr, xss, xrs, lss, lrs,
):
    g = lax.axis_index("group")
    e = lax.axis_index("expert")
    x, yl, c = g // 4, (g // 2) % 2, g % 2
    yh, z = e // NZ, e % NZ

    def at(dx=0, dyl=0, dc=0, dyh=0, dz=0):
        xx = mod(x + dx, NX)
        yy = 1 - yl if dyl else yl
        cc = 1 - c if dc else c
        return ((xx * 2 + yy) * 2 + cc, mod(yh + dyh, NYH) * NZ + mod(z + dz, NZ))

    def rc(src, dst, ss, rs, dev):
        return pltpu.make_async_remote_copy(src, dst, ss, rs, device_id=dev, device_id_type=MESH)

    sends = []

    def go(cp):
        cp.start()
        sends.append(cp)
        return cp

    bar = pltpu.get_barrier_semaphore()
    peers = [at(dyh=1), at(dyh=2), at(dyh=3), at(dz=1), at(dz=-1), at(dx=1), at(dx=-1), at(dyl=1), at(dc=1)]
    for p in peers:
        pl.semaphore_signal(bar, inc=1, device_id=p, device_id_type=MESH)
    cp_t = pltpu.make_async_copy(tok_hbm.at[0], td.at[0], in_sem.at[0])
    cp_d = pltpu.make_async_copy(dy_hbm.at[0], td.at[1], in_sem.at[1])
    cp_t.start()
    cp_d.start()

    W[g, :, 0:HD] = gw_ref[...]
    W[g, :, HD:2 * HD] = uw_ref[...]
    W[g, :, 2 * HD:3 * HD] = dw_ref[...]

    pl.semaphore_wait(bar, len(peers))

    def wid(dx=0, dyl=0, dc=0):
        return at(dx=dx, dyl=dyl, dc=dc)[0]

    cp_wl = go(rc(W.at[g], W.at[g], wl.at[0], wl.at[1], at(dyl=1)))

    def wx1(st, sgn):
        i = wid(dyl=st)
        d = 0 if sgn > 0 else 1
        return rc(W.at[i], W.at[i], wxs.at[d, 0, st], wxr.at[d, 0, st], at(dx=sgn))

    def wx2(st, sgn):
        d = 0 if sgn > 0 else 1
        i = wid(dx=-sgn, dyl=st)
        h = DB // 2
        lo = 0 if sgn > 0 else h
        return rc(W.at[i, lo:lo + h], W.at[i, lo:lo + h], wxs.at[d, 1, st], wxr.at[d, 1, st], at(dx=sgn))

    def wcore(dx, st):
        i = wid(dx=dx, dyl=st)
        k = (dx % 4) * 2 + st
        return rc(W.at[i], W.at[i], wcs.at[k], wcr.at[k], at(dc=1))

    w1 = {(st, sg): wx1(st, sg) for st in (0, 1) for sg in (1, -1)}
    w2 = {(st, sg): wx2(st, sg) for st in (0, 1) for sg in (1, -1)}
    wc = {(dx, st): wcore(dx, st) for dx in (0, 1, 2, 3) for st in (0, 1)}

    go(w1[0, 1])
    go(w1[0, -1])
    go(wc[0, 0])

    n = 2 * SLOT * Q
    r_i = lax.broadcasted_iota(jnp.int32, (n, 2 * TOK), 0)
    k_i = lax.broadcasted_iota(jnp.int32, (n, 2 * TOK), 1)
    q_i = r_i // (2 * SLOT)
    ts = r_i - q_i * (2 * SLOT)
    want = jnp.full((n, 2 * TOK), -1, jnp.int32)
    cnt = cnt_ref[0, 0]
    for s in range(SLOT):
        p = jnp.where(s < cnt, row_ref[0, s], -TOK - 1)
        want = jnp.where(ts == s, p, want)
        want = jnp.where(ts == SLOT + s, p + TOK, want)
    hit = (want == k_i) & (want >= jnp.where(ts < SLOT, 0, TOK))
    cp_t.wait()
    cp_d.wait()
    acc = jnp.zeros((n, QW), F32)
    for q in range(Q):
        eq = jnp.where(hit & (q_i == q), 1.0, 0.0).astype(BF)
        both = jnp.concatenate([td[0, :, q * QW:(q + 1) * QW], td[1, :, q * QW:(q + 1) * QW]], axis=0)
        acc = acc + jnp.dot(eq, both, preferred_element_type=F32)
    Z[0, 0] = acc.astype(BF)

    HB = n // 2

    def zc(k, u, sgn):
        d = 0 if sgn > 0 else 1
        src = (-sgn * (k - 1)) % NZ
        dst = (-sgn * k) % NZ
        if k == 4:
            lo = 0 if sgn > 0 else HB
            return rc(Z.at[src, u, lo:lo + HB], Z.at[dst, u, lo:lo + HB], zss.at[d, k - 1, u], zrs.at[d, k - 1, u], at(dz=sgn))
        return rc(Z.at[src, u], Z.at[dst, u], zss.at[d, k - 1, u], zrs.at[d, k - 1, u], at(dz=sgn))

    zz = {(k, u, sg): zc(k, u, sg) for k in (1, 2, 3, 4) for u in range(NYH) for sg in (1, -1)}

    def zsend(k, u):
        go(zz[k, u, 1])
        go(zz[k, u, -1])

    def zwait(k, u):
        zz[k, u, 1].wait_recv()
        zz[k, u, -1].wait_recv()

    def zstep(k, u):
        zwait(k, u)
        if k < 4:
            zsend(k + 1, u)

    yc = {u: rc(Z.at[0, 0], Z.at[0, (-u) % NYH], yss.at[u], yrs.at[(-u) % NYH], at(dyh=u)) for u in (1, 2, 3)}
    zsend(1, 0)
    go(yc[1])
    go(yc[3])
    go(yc[2])

    def ywait(u):
        yc[(-u) % NYH].wait_recv()

    ywait(1)
    zsend(1, 1)
    ywait(3)
    zsend(1, 3)
    zstep(1, 0)
    for sg in (1, -1):
        w1[0, sg].wait_recv()
        go(w2[0, sg])
        go(wc[(-sg) % 4, 0])
    cp_wl.wait_recv()
    go(w1[1, 1])
    go(w1[1, -1])
    go(wc[0, 1])
    ywait(2)
    zsend(1, 2)
    zstep(1, 1)
    zstep(1, 3)
    zstep(2, 0)
    zstep(1, 2)
    for sg in (1, -1):
        w2[0, sg].wait_recv()
    go(wc[2, 0])
    for sg in (1, -1):
        w1[1, sg].wait_recv()
        go(w2[1, sg])
        go(wc[(-sg) % 4, 1])

    def permute(zr):
        src = Z[zr].reshape(NYH * n, QW)
        out = jnp.dot(gp_ref[...], src, preferred_element_type=F32).astype(BF)
        for q in range(Q):
            R[zr * 48:(zr + 1) * 48, q * QW:(q + 1) * QW] = out[q * 48:(q + 1) * 48]

    def forward(zrs_):
        m = 48 * len(zrs_)

        def rows(i):
            ln = pl.ds(pl.multiple_of(i * DB, DB), DB)
            return jnp.concatenate([R[zr * 48:(zr + 1) * 48, ln] for zr in zrs_], axis=0)

        def body(i, acc):
            return acc + jnp.dot(rows(i), W[i], preferred_element_type=F32)

        pre = lax.fori_loop(0, 16, body, jnp.zeros((m, 3 * HD), F32))
        for k, zr in enumerate(zrs_):
            b = k * 48
            gate = pre[b:b + 24, 0:HD]
            up = pre[b:b + 24, HD:2 * HD]
            gh = pre[b + 24:b + 48, 2 * HD:]
            sg = 1.0 / (1.0 + jnp.exp(-gate))
            act = gate * sg
            r0 = zr * 48
            d_gate = gh * up * sg * (1.0 + gate * (1.0 - sg))
            d_up = gh * act
            J[zr, :, 0:HD] = d_gate
            J[zr, :, HD:2 * HD] = d_up
            A[r0:r0 + 24, 0:HD] = d_gate
            A[r0:r0 + 24, HD:2 * HD] = d_up
            A[r0:r0 + 24, 2 * HD:] = jnp.zeros((24, HD), F32)
            A[r0 + 24:r0 + 48, 0:2 * HD] = jnp.zeros((24, 2 * HD), F32)
            A[r0 + 24:r0 + 48, 2 * HD:] = act * up

    permute(0)
    zstep(2, 1)
    zstep(2, 3)
    zstep(3, 0)
    permute(1)
    permute(7)
    zstep(2, 2)
    for sg in (1, -1):
        w2[1, sg].wait_recv()
    go(wc[2, 1])
    zstep(3, 1)
    zstep(3, 3)
    permute(2)
    permute(6)
    for cpw in wc.values():
        cpw.wait_recv()
    zstep(3, 2)
    forward([0, 1, 7])
    forward([2, 6])
    permute(3)
    permute(5)
    forward([3, 5])
    zwait(4, 0)
    zwait(4, 1)
    zwait(4, 3)
    zwait(4, 2)
    permute(4)
    forward([4])

    def row_grad(zrs_):
        j = jnp.concatenate([J[zr] for zr in zrs_], axis=0).astype(BF)

        def body(q, carry):
            w = W[pl.ds(2 * q, 2), :, 0:2 * HD].reshape(QW, 2 * HD)
            res = lax.dot_general(j, w, (((1,), (1,)), ((), ())), preferred_element_type=F32)
            for k, zr in enumerate(zrs_):
                PP[zr, pl.ds(pl.multiple_of(q * ROWS, 8), ROWS), :] = res[k * ROWS:(k + 1) * ROWS]
            return carry

        lax.fori_loop(0, Q, body, 0)

    def rz(k, cc, sgn):
        d = 0 if sgn > 0 else 1
        return rc(ZS.at[d, k - 1, cc], ZR.at[d, k - 1, cc], rzs.at[d, k - 1, cc], rzr.at[d, k - 1, cc], at(dz=sgn))

    far = {1: (0, 1), -1: (2, 3)}
    order = {1: (2, 3, 0, 1), -1: (0, 1, 2, 3)}
    rzc = {}
    for sg in (1, -1):
        for k in (1, 2, 3, 4):
            for cc in (far[sg] if k == 1 else range(CH)):
                rzc[k, cc, sg] = rz(k, cc, sg)

    def lanes(cc):
        return slice(cc * CW, (cc + 1) * CW)

    def rz_hop(k):
        for i in range(CH):
            for sg in (1, -1):
                d = 0 if sg > 0 else 1
                zr = (sg * (5 - k)) % NZ
                if k == 1:
                    if i >= 2:
                        continue
                    cc = far[sg][i]
                    val = PP[zr, :, lanes(cc)]
                else:
                    cc = order[sg][i]
                    val = PP[zr, :, lanes(cc)]
                    if k > 2 or cc in far[sg]:
                        rzc[k - 1, cc, sg].wait_recv()
                        val = val + ZR[d, k - 2, cc].astype(F32)
                ZS[d, k - 1, cc] = val.astype(BF)
                go(rzc[k, cc, sg])

    row_grad([4])
    rz_hop(1)

    AT[...] = A[...].T.astype(BF)

    def wgrad(dx, st, dc):
        i = wid(dx=dx, dyl=st, dc=dc)
        ln = pl.ds(pl.multiple_of(i * DB, DB), DB)
        return jnp.dot(AT[...], R[:, ln], preferred_element_type=F32)

    ec = {dx: rc(ES.at[dx], ER.at[dx], ecs.at[dx], ecr.at[dx], at(dc=1)) for dx in range(4)}

    def other_core(dx):
        for st in (0, 1):
            ES[dx, st] = wgrad(dx, st, 1).astype(BF)
        go(ec[dx])

    def own_core(dx):
        for st in (0, 1):
            SS[dx, st] = wgrad(dx, st, 0)

    other_core(2)
    row_grad([3, 5])
    own_core(2)
    rz_hop(2)
    row_grad([2, 6])

    xc = {}
    for sg in (1, -1):
        d = 0 if sg > 0 else 1
        for it in range(3):
            xc[sg, it] = rc(XS.at[d, it], XR.at[d, it], xss.at[d, it], xrs.at[d, it], at(dx=sg))
    far_st = {1: 1, -1: 0}

    ec[2].wait_recv()
    for sg in (1, -1):
        d = 0 if sg > 0 else 1
        st = far_st[sg]
        XS[d, 0] = (SS[2, st] + ER[2, st].astype(F32)).astype(BF)
        go(xc[sg, 0])
    other_core(1)
    own_core(1)
    rz_hop(3)
    row_grad([1, 7])
    other_core(3)
    own_core(3)
    for sg in (1, -1):
        d = 0 if sg > 0 else 1
        st = 1 - far_st[sg]
        dx = sg % 4
        ec[dx].wait_recv()
        XS[d, 1] = (SS[dx, st] + ER[dx, st].astype(F32)).astype(BF)
        go(xc[sg, 1])
    rz_hop(4)
    row_grad([0])
    for sg in (1, -1):
        d = 0 if sg > 0 else 1
        st = far_st[sg]
        dx = sg % 4
        xc[sg, 0].wait_recv()
        XS[d, 2] = (SS[dx, st] + ER[dx, st].astype(F32) + XR[d, 0].astype(F32)).astype(BF)
        go(xc[sg, 2])
    other_core(0)
    own_core(0)

    ry = {(u, cc): rc(Y0.at[u, cc], YR.at[(-u) % NYH, cc], rys.at[u, cc], ryr.at[(-u) % NYH, cc], at(dyh=u)) for u in (1, 2, 3) for cc in range(CH)}
    for cc in (2, 3, 0, 1):
        rzc[4, cc, 1].wait_recv()
        rzc[4, cc, -1].wait_recv()
        tot = PP[0, :, lanes(cc)] + ZR[0, 3, cc].astype(F32) + ZR[1, 3, cc].astype(F32)
        out = jnp.dot(sp_ref[...], tot.astype(BF), preferred_element_type=F32).astype(BF)
        for u in range(NYH):
            Y0[u, cc] = out[u * 48:(u + 1) * 48]
        for u in (2, 1, 3):
            go(ry[u, cc])

    ec[0].wait_recv()
    cp_l = rc(LS, LR, lss.at[0], lrs.at[0], at(dyl=1))
    xc[1, 1].wait_recv()
    xc[-1, 1].wait_recv()
    xc[1, 2].wait_recv()
    LS[...] = (SS[0, 1] + ER[0, 1].astype(F32) + XR[0, 2].astype(F32) + XR[1, 1].astype(F32)).astype(BF)
    go(cp_l)
    xc[-1, 2].wait_recv()
    own = SS[0, 0] + ER[0, 0].astype(F32) + XR[0, 1].astype(F32) + XR[1, 2].astype(F32)
    SS[0, 0] = own

    o_t = lax.broadcasted_iota(jnp.int32, (TOK, Q * SLOT), 0)
    o_r = lax.broadcasted_iota(jnp.int32, (TOK, Q * SLOT), 1)
    o_q = o_r // SLOT
    o_s = o_r - o_q * SLOT
    row_of = jnp.full((TOK, Q * SLOT), -1, jnp.int32)
    for s in range(SLOT):
        row_of = jnp.where(o_s == s, jnp.where(s < cnt, row_ref[0, s], -1), row_of)
    place = row_of == o_t
    for cc in range(CH):
        for u in (1, 2, 3):
            ry[u, cc].wait_recv()
    fin = []
    for cc in range(CH):
        fin.append(Y0[0, cc].astype(F32) + YR[1, cc].astype(F32) + YR[2, cc].astype(F32) + YR[3, cc].astype(F32))
    fin = jnp.concatenate(fin, axis=1).astype(BF)
    for q in range(Q):
        oh = jnp.where(place & (o_q == q), 1.0, 0.0).astype(BF)
        gt_ref[0, :, q * QW:(q + 1) * QW] = jnp.dot(oh, fin, preferred_element_type=F32).astype(BF)

    cp_l.wait_recv()
    tot = (SS[0, 0] + LR[...].astype(F32)) * (1.0 / 16.0)
    gg_ref[...] = tot[0:HD].T.astype(BF)
    gu_ref[...] = tot[HD:2 * HD].T.astype(BF)
    gd_ref[...] = tot[2 * HD:].T.astype(BF)

    for cp in sends:
        cp.wait_send()


def local(tokens, grad_out, gate_w, up_w, down_w, take_count, take_rows):
    vm = pl.BlockSpec(memory_space=pltpu.VMEM)
    sm = pl.BlockSpec(memory_space=pltpu.SMEM)
    hb = pl.BlockSpec(memory_space=pl.ANY)
    dma = pltpu.SemaphoreType.DMA
    n = 2 * SLOT * Q
    return pl.pallas_call(
        kernel,
        out_shape=(
            jax.ShapeDtypeStruct((1, TOK, D), BF),
            jax.ShapeDtypeStruct((DB, HD), BF),
            jax.ShapeDtypeStruct((DB, HD), BF),
            jax.ShapeDtypeStruct((DB, HD), BF),
        ),
        in_specs=[hb, hb, vm, vm, vm, sm, sm, vm, vm],
        out_specs=(vm, vm, vm, vm),
        scratch_shapes=[
            pltpu.VMEM((2, TOK, D), BF),
            pltpu.VMEM((NZ, NYH, n, QW), BF),
            pltpu.VMEM((NZ * 48, D), BF),
            pltpu.VMEM((16, DB, 3 * HD), BF),
            pltpu.VMEM((8, 128), F32),
            pltpu.VMEM((NZ * 48, 3 * HD), F32),
            pltpu.VMEM((3 * HD, NZ * 48), BF),
            pltpu.VMEM((NZ, ROWS, 2 * HD), F32),
            pltpu.VMEM((NZ, Q * ROWS, QW), F32),
            pltpu.VMEM((NYH, CH, Q * SLOT, CW), BF),
            pltpu.VMEM((NYH, CH, Q * SLOT, CW), BF),
            pltpu.VMEM((2, 4, CH, Q * ROWS, CW), BF),
            pltpu.VMEM((2, 4, CH, Q * ROWS, CW), BF),
            pltpu.VMEM((NX, 2, 3 * HD, DB), F32),
            pltpu.VMEM((NX, 2, 3 * HD, DB), BF),
            pltpu.VMEM((NX, 2, 3 * HD, DB), BF),
            pltpu.VMEM((2, 3, 3 * HD, DB), BF),
            pltpu.VMEM((2, 3, 3 * HD, DB), BF),
            pltpu.VMEM((3 * HD, DB), BF),
            pltpu.VMEM((3 * HD, DB), BF),
            dma((2,)),
            dma((2, 4, NYH)), dma((2, 4, NYH)),
            dma((NYH,)), dma((NYH,)),
            dma((2,)),
            dma((2, 2, 2)), dma((2, 2, 2)),
            dma((8,)), dma((8,)),
            dma((2, 4, CH)), dma((2, 4, CH)),
            dma((NYH, CH)), dma((NYH, CH)),
            dma((NX,)), dma((NX,)),
            dma((2, 3)), dma((2, 3)),
            dma((1,)), dma((1,)),
        ],
        compiler_params=pltpu.CompilerParams(
            collective_id=0, has_side_effects=True, vmem_limit_bytes=56 * 2 ** 20
        ),
        cost_estimate=pl.CostEstimate(flops=2 * 10 ** 9, bytes_accessed=4 * 2 ** 20, transcendentals=0),
    )(
        tokens, grad_out, gate_w, up_w, down_w, take_count, take_rows.reshape(1, SLOT),
        jnp.asarray(gather_perm(), BF), jnp.asarray(scatter_perm(), BF),
    )


def solution(mesh):
    rows = P("group", "expert", None)
    flat = P("group", "expert")
    return jax.shard_map(
        local,
        mesh=mesh,
        in_specs=(rows, rows, flat, flat, flat, flat, rows),
        out_specs=(rows, flat, flat, flat),
        check_vma=False,
    )
```

```python
import heapq

import jax
import jax.numpy as jnp
import numpy as np
from jax import lax
from jax.experimental import pallas as pl
from jax.experimental.pallas import tpu as pltpu
from jax.sharding import PartitionSpec as P

BF = jnp.bfloat16
F32 = jnp.float32
SLOT = 6
NX, NYH, NZ = 4, 4, 8
TOK = 128
D = 4096
HD = 128
DB = 256
Q = 8
QW = D // Q
ROWS = NYH * SLOT
CH = 4
CW = QW // CH
MESH = pl.DeviceIdType.MESH
POS = {0: 0, 1: 1, 7: 2, 2: 3, 6: 4, 3: 5, 5: 6, 4: 7}
GROUPS = ((0,), (1, 7), (2, 6), (3, 5), (4,))


def mod(a, n):
    return lax.rem(a + n, n)


def gather_perm():
    n = NYH * Q * 2 * SLOT
    m = np.zeros((n, n), np.float32)
    for u in range(NYH):
        for q in range(Q):
            for t in range(2):
                for s in range(SLOT):
                    m[((q * 2 + t) * NYH + u) * SLOT + s, ((u * Q + q) * 2 + t) * SLOT + s] = 1
    return m


def scatter_perm():
    n = NYH * Q * SLOT
    m = np.zeros((n, n), np.float32)
    for u in range(NYH):
        for q in range(Q):
            for s in range(SLOT):
                m[(u * Q + q) * SLOT + s, (q * NYH + u) * SLOT + s] = 1
    return m


def gather_plan():
    unit = 0.87
    free = {}
    heap = []
    order = []
    got = {}
    need = {zr: 8 for zr in range(NZ)}
    need[0] = 6
    weights_left = 17
    tasks = []
    done = set()

    def send(t, key, link, length, lat):
        start = max(t, free.get(link, 0.0))
        free[link] = start + length
        heapq.heappush(heap, (start + length + lat, len(order), key))
        order.append(("send", key))

    def z_send(t, k, u, h, sg):
        send(t, ("z", k, u, h, sg), ("z", sg), unit, 2.5)

    def far_send(t, zr, sg):
        send(t, ("f", zr, sg), ("y", sg), 2 * unit, 2.8)

    def passes(t, zr, u, h):
        if u == 1 and h == 0:
            far_send(t, zr, -1)
        if u == 3 and h == 1:
            far_send(t, zr, 1)

    def core_send(t, dx, st):
        send(t, ("wc", dx, st), "core", 0.7, 0.9)

    for h in (0, 1):
        for sg in (1, -1):
            send(0, ("y", (-sg) % NYH, h), ("y", sg), 2 * unit, 2.8)
        for sg in (1, -1):
            z_send(0, 1, 0, h, sg)
    for sg in (1, -1):
        send(0, ("w1", 0, sg), ("x", sg), 3.5, 2.5)
    core_send(0, 0, 0)
    send(0, ("wl",), ("y", 1), 3.5, 2.5)

    t = 0.0
    while heap or tasks:
        if heap and heap[0][0] <= t + 0.2 or not tasks:
            at, _, key = heapq.heappop(heap)
            t = max(t, at) + 0.1
            order.append(("wait", key))
            kind = key[0]
            zr = None
            if kind == "y":
                _, u, h = key
                zr = 0
                for sg in (1, -1):
                    z_send(t, 1, u, h, sg)
                passes(t, 0, u, h)
            elif kind == "z":
                _, k, u, h, sg = key
                zr = (-sg * k) % NZ
                if k < 3 or (k == 3 and h == (0 if sg > 0 else 1)):
                    z_send(t, k + 1, u, h, sg)
                passes(t, zr, u, h)
            elif kind == "f":
                zr = key[1]
            else:
                weights_left -= 1
                if kind == "wl":
                    for sg in (1, -1):
                        send(t, ("w1", 1, sg), ("x", sg), 3.5, 2.5)
                    core_send(t, 0, 1)
                elif kind == "w1":
                    _, st, sg = key
                    send(t, ("w2", st, sg), ("x", sg), 1.75, 2.5)
                    core_send(t, (-sg) % NX, st)
                elif kind == "w2":
                    got[key[:2]] = got.get(key[:2], 0) + 1
                    if got[key[:2]] == 2:
                        core_send(t, 2, key[1])
            if zr is not None:
                got[zr] = got.get(zr, 0) + 1
                if got[zr] == need[zr]:
                    tasks.append(("permute", zr))
        else:
            task = tasks.pop(0)
            order.append(task)
            t += 0.6 if task[0] == "permute" else 1.5
            done.add(task)
            if task[0] == "forward":
                tasks.append(("rows", task[1]))
        for grp in GROUPS:
            if weights_left == 0 and ("forward", grp) not in done and ("forward", grp) not in tasks:
                if all(("permute", zr) in done for zr in grp):
                    tasks.append(("forward", grp))
    return order


def kernel(
    tok_hbm, dy_hbm, gw_ref, uw_ref, dw_ref, cnt_ref, row_ref, gp_ref, sp_ref,
    fin_ref, wg_ref,
    td, Z, RX, RD, W, J, H, JT, HT, PP, Y0, YR, ZS, ZR, SS, ES, ER, XS, XR, LS, LR,
    in_sem, zss, zrs, yss, yrs, fss, frs, wl, wxs, wxr, wcs, wcr, rzs, rzr, rys, ryr, ecs, ecr, xss, xrs, lss, lrs,
):
    g = lax.axis_index("group")
    e = lax.axis_index("expert")
    x, yl, c = g // 4, (g // 2) % 2, g % 2
    yh, z = e // NZ, e % NZ

    def at(dx=0, dyl=0, dc=0, dyh=0, dz=0):
        xx = mod(x + dx, NX)
        yy = 1 - yl if dyl else yl
        cc = 1 - c if dc else c
        return ((xx * 2 + yy) * 2 + cc, mod(yh + dyh, NYH) * NZ + mod(z + dz, NZ))

    def rc(src, dst, ss, rs, dev):
        return pltpu.make_async_remote_copy(src, dst, ss, rs, device_id=dev, device_id_type=MESH)

    sends = []

    def go(cp):
        cp.start()
        sends.append(cp)

    bar = pltpu.get_barrier_semaphore()
    peers = [at(dyh=1), at(dyh=2), at(dyh=3), at(dz=1), at(dz=-1), at(dx=1), at(dx=-1), at(dyl=1), at(dc=1)]
    for p in peers:
        pl.semaphore_signal(bar, inc=1, device_id=p, device_id_type=MESH)
    cp_t = pltpu.make_async_copy(tok_hbm.at[0], td.at[0:TOK], in_sem.at[0])
    cp_d = pltpu.make_async_copy(dy_hbm.at[0], td.at[TOK:2 * TOK], in_sem.at[1])
    cp_t.start()
    cp_d.start()

    def wid(dx=0, dyl=0, dc=0):
        return at(dx=dx, dyl=dyl, dc=dc)[0]

    def wrows(i, lo=0, n=DB):
        return pl.ds(pl.multiple_of(i * DB + lo, n), n)

    W[wrows(g), 0:HD] = gw_ref[...]
    W[wrows(g), HD:2 * HD] = uw_ref[...]
    W[wrows(g), 2 * HD:3 * HD] = dw_ref[...]

    n = 2 * SLOT * Q
    HB = n // 2
    r_i = lax.broadcasted_iota(jnp.int32, (n, 2 * TOK), 0)
    k_i = lax.broadcasted_iota(jnp.int32, (n, 2 * TOK), 1)
    q_i = r_i // (2 * SLOT)
    ts = r_i - q_i * (2 * SLOT)
    want = jnp.full((n, 2 * TOK), -1, jnp.int32)
    cnt = cnt_ref[0, 0]
    for s in range(SLOT):
        p = jnp.where(s < cnt, row_ref[0, s], -TOK - 1)
        want = jnp.where(ts == s, p, want)
        want = jnp.where(ts == SLOT + s, p + TOK, want)
    hit = (want == k_i) & (want >= jnp.where(ts < SLOT, 0, TOK))
    cp_t.wait()
    cp_d.wait()
    acc = jnp.zeros((n, QW), F32)
    for q in range(Q):
        eq = jnp.where(hit & (q_i == q), 1.0, 0.0).astype(BF)
        acc = acc + jnp.dot(eq, td[:, q * QW:(q + 1) * QW], preferred_element_type=F32)
    Z[0, 0] = acc.astype(BF)

    pl.semaphore_wait(bar, len(peers))

    def half(h):
        return slice(h * HB, (h + 1) * HB)

    def dirn(sg):
        return 0 if sg > 0 else 1

    cps = {}
    for sg in (1, -1):
        d = dirn(sg)
        for h in (0, 1):
            u = (-sg) % NYH
            cps["y", u, h] = rc(Z.at[0, 0, half(h)], Z.at[0, u, half(h)], yss.at[u, h], yrs.at[u, h], at(dyh=sg))
            for k in (1, 2, 3, 4):
                if k == 4 and h != d:
                    continue
                for u in (0, 1, 3):
                    src, dst = (-sg * (k - 1)) % NZ, (-sg * k) % NZ
                    cps["z", k, u, h, sg] = rc(
                        Z.at[src, u, half(h)], Z.at[dst, u, half(h)],
                        zss.at[d, k - 1, u, h], zrs.at[d, k - 1, u, h], at(dz=sg),
                    )
        for zr in range(NZ):
            u, h = (3, 1) if sg > 0 else (1, 0)
            cps["f", zr, sg] = rc(
                Z.at[zr, u, half(h)], Z.at[zr, 2, half(h)], fss.at[zr, d], frs.at[zr, d], at(dyh=sg)
            )
        for st in (0, 1):
            r = wrows(wid(dyl=st))
            cps["w1", st, sg] = rc(W.at[r], W.at[r], wxs.at[d, 0, st], wxr.at[d, 0, st], at(dx=sg))
            r = wrows(wid(dx=-sg, dyl=st), d * (DB // 2), DB // 2)
            cps["w2", st, sg] = rc(W.at[r], W.at[r], wxs.at[d, 1, st], wxr.at[d, 1, st], at(dx=sg))
    cps["wl",] = rc(W.at[wrows(g)], W.at[wrows(g)], wl.at[0], wl.at[1], at(dyl=1))
    for dx in range(NX):
        for st in (0, 1):
            r = wrows(wid(dx=dx, dyl=st))
            cps["wc", dx, st] = rc(W.at[r], W.at[r], wcs.at[dx * 2 + st], wcr.at[dx * 2 + st], at(dc=1))

    def permute(zr):
        src = Z[zr].reshape(NYH * n, QW)
        out = jnp.dot(gp_ref[...], src, preferred_element_type=F32).astype(BF)
        r0 = POS[zr] * ROWS
        for q in range(Q):
            RX[r0:r0 + ROWS, q * QW:(q + 1) * QW] = out[q * 48:q * 48 + 24]
            RD[r0:r0 + ROWS, q * QW:(q + 1) * QW] = out[q * 48 + 24:q * 48 + 48]

    def group_rows(grp):
        return slice(POS[grp[0]] * ROWS, (POS[grp[-1]] + 1) * ROWS)

    def forward(grp):
        r = group_rows(grp)
        pre = jnp.dot(RX[r], W[:, 0:2 * HD], preferred_element_type=F32)
        gh = jnp.dot(RD[r], W[:, 2 * HD:], preferred_element_type=F32)
        gate = pre[:, 0:HD]
        up = pre[:, HD:]
        sg = 1.0 / (1.0 + jnp.exp(-gate))
        act = gate * sg
        J[r, 0:HD] = gh * up * sg * (1.0 + gate * (1.0 - sg))
        J[r, HD:] = gh * act
        H[r] = act * up

    def row_grad(grp):
        j = J[group_rows(grp)].astype(BF)
        for q in range(Q):
            res = lax.dot_general(
                j, W[q * QW:(q + 1) * QW, 0:2 * HD], (((1,), (1,)), ((), ())), preferred_element_type=F32
            )
            for k, zr in enumerate(grp):
                PP[zr, q * ROWS:(q + 1) * ROWS, :] = res[k * ROWS:(k + 1) * ROWS]

    for step in gather_plan():
        what, arg = step
        if what == "send":
            go(cps[arg])
        elif what == "wait":
            cps[arg].wait_recv()
        elif what == "permute":
            permute(arg)
        elif what == "forward":
            forward(arg)
        else:
            row_grad(arg)

    def lanes(cc):
        return slice(cc * CW, (cc + 1) * CW)

    far = {1: (0, 1), -1: (2, 3)}
    order = {1: (2, 3, 0, 1), -1: (0, 1, 2, 3)}
    rzc = {}
    for sg in (1, -1):
        d = dirn(sg)
        for k in (1, 2, 3, 4):
            for cc in (far[sg] if k == 1 else range(CH)):
                rzc[k, cc, sg] = rc(
                    ZS.at[d, k - 1, cc], ZR.at[d, k - 1, cc], rzs.at[d, k - 1, cc], rzr.at[d, k - 1, cc], at(dz=sg)
                )

    def rz_hop(k):
        for i in range(CH):
            for sg in (1, -1):
                d = dirn(sg)
                zr = (sg * (5 - k)) % NZ
                if k == 1:
                    if i >= 2:
                        continue
                    cc = far[sg][i]
                    val = PP[zr, :, lanes(cc)]
                else:
                    cc = order[sg][i]
                    val = PP[zr, :, lanes(cc)]
                    if k > 2 or cc in far[sg]:
                        rzc[k - 1, cc, sg].wait_recv()
                        val = val + ZR[d, k - 2, cc].astype(F32)
                ZS[d, k - 1, cc] = val.astype(BF)
                go(rzc[k, cc, sg])

    rz_hop(1)

    JT[...] = J[...].T.astype(BF)
    HT[...] = H[...].T.astype(BF)
    ec = {dx: rc(ES.at[dx], ER.at[dx], ecs.at[dx], ecr.at[dx], at(dc=1)) for dx in range(NX)}

    def wgrad(dst, dx, st, dc):
        i = wid(dx=dx, dyl=st, dc=dc)
        ln = pl.ds(pl.multiple_of(i * DB, DB), DB)
        dst[dx, st, 0:2 * HD] = jnp.dot(JT[...], RX[:, ln], preferred_element_type=F32).astype(dst.dtype)
        dst[dx, st, 2 * HD:] = jnp.dot(HT[...], RD[:, ln], preferred_element_type=F32).astype(dst.dtype)

    def other_core(dx):
        for st in (0, 1):
            wgrad(ES, dx, st, 1)
        go(ec[dx])

    def own_core(dx):
        for st in (0, 1):
            wgrad(SS, dx, st, 0)

    WH = 3 * HD // 2
    xc = {}
    for sg in (1, -1):
        for it in range(6):
            d = dirn(sg)
            xc[sg, it] = rc(XS.at[d, it], XR.at[d, it], xss.at[d, it], xrs.at[d, it], at(dx=sg))

    def piece(sg, it):
        d = dirn(sg)
        st = (1, 0, 1, 1, 0, 0)[it]
        h = 1 - d if it in (2, 4) else d
        dx = 2 if it < 2 else sg % NX
        hs = slice(h * WH, (h + 1) * WH)
        val = SS[dx, st, hs] + ER[dx, st, hs].astype(F32)
        if it in (3, 5):
            prev = 0 if it == 3 else 1
            xc[sg, prev].wait_recv()
            val = val + XR[d, prev].astype(F32)
        XS[d, it] = val.astype(BF)
        go(xc[sg, it])

    def both_ways(it):
        piece(1, it)
        piece(-1, it)

    other_core(2)
    own_core(2)
    rz_hop(2)
    ec[2].wait_recv()
    both_ways(0)
    both_ways(1)
    other_core(1)
    other_core(3)
    rz_hop(3)
    own_core(1)
    own_core(3)
    ec[1].wait_recv()
    ec[3].wait_recv()
    both_ways(2)
    rz_hop(4)
    both_ways(3)
    both_ways(4)
    other_core(0)
    own_core(0)
    both_ways(5)

    ry = {
        (u, cc): rc(Y0.at[u, cc], YR.at[(-u) % NYH, cc], rys.at[u, cc], ryr.at[(-u) % NYH, cc], at(dyh=u))
        for u in (1, 2, 3) for cc in range(CH)
    }
    for cc in (2, 0, 3, 1):
        rzc[4, cc, 1].wait_recv()
        rzc[4, cc, -1].wait_recv()
        tot = PP[0, :, lanes(cc)] + ZR[0, 3, cc].astype(F32) + ZR[1, 3, cc].astype(F32)
        out = jnp.dot(sp_ref[...], tot.astype(BF), preferred_element_type=F32).astype(BF)
        for u in range(NYH):
            Y0[u, cc] = out[u * 48:(u + 1) * 48]
        for u in (2, 1, 3):
            go(ry[u, cc])

    ec[0].wait_recv()

    def x_total(st, h):
        hs = slice(h * WH, (h + 1) * WH)
        val = SS[0, st, hs] + ER[0, st, hs].astype(F32)
        for sg in (1, -1):
            d = dirn(sg)
            it = (2 if st else 4) + (1 if h == d else 0)
            xc[sg, it].wait_recv()
            val = val + XR[d, it].astype(F32)
        return val

    lc = [rc(LS.at[h], LR.at[h], lss.at[h], lrs.at[h], at(dyl=1)) for h in (0, 1)]
    for h in (0, 1):
        LS[h] = x_total(1, h).astype(BF)
        go(lc[h])
    for h in (0, 1):
        SS[1, 0, h * WH:(h + 1) * WH] = x_total(0, h)

    for cc in range(CH):
        for u in (1, 2, 3):
            ry[u, cc].wait_recv()
        fin_ref[:, lanes(cc)] = (
            Y0[0, cc].astype(F32) + YR[1, cc].astype(F32) + YR[2, cc].astype(F32) + YR[3, cc].astype(F32)
        ).astype(BF)
    for h in (0, 1):
        hs = slice(h * WH, (h + 1) * WH)
        lc[h].wait_recv()
        wg_ref[hs] = ((SS[1, 0, hs] + LR[h].astype(F32)) * (1.0 / 16.0)).astype(BF)

    for cp in sends:
        cp.wait_send()


def finish(cnt_ref, row_ref, fin_ref, wg_ref, gt_ref, gg_ref, gu_ref, gd_ref):
    cnt = cnt_ref[0, 0]
    o_t = lax.broadcasted_iota(jnp.int32, (TOK, Q * SLOT), 0)
    o_r = lax.broadcasted_iota(jnp.int32, (TOK, Q * SLOT), 1)
    o_q = o_r // SLOT
    o_s = o_r - o_q * SLOT
    row_of = jnp.full((TOK, Q * SLOT), -1, jnp.int32)
    for s in range(SLOT):
        row_of = jnp.where(o_s == s, jnp.where(s < cnt, row_ref[0, s], -1), row_of)
    place = row_of == o_t
    for q in range(Q):
        oh = jnp.where(place & (o_q == q), 1.0, 0.0).astype(BF)
        gt_ref[0, :, q * QW:(q + 1) * QW] = jnp.dot(oh, fin_ref[...], preferred_element_type=F32).astype(BF)
    for k, ref in enumerate((gg_ref, gu_ref, gd_ref)):
        ref[...] = wg_ref[k * HD:(k + 1) * HD].astype(F32).T.astype(BF)


def local(tokens, grad_out, gate_w, up_w, down_w, take_count, take_rows):
    vm = pl.BlockSpec(memory_space=pltpu.VMEM)
    sm = pl.BlockSpec(memory_space=pltpu.SMEM)
    hb = pl.BlockSpec(memory_space=pl.ANY)
    dma = pltpu.SemaphoreType.DMA
    n = 2 * SLOT * Q
    WH = 3 * HD // 2
    picked = take_rows.reshape(1, SLOT)
    fin, wg = pl.pallas_call(
        kernel,
        out_shape=(
            jax.ShapeDtypeStruct((Q * SLOT, QW), BF),
            jax.ShapeDtypeStruct((3 * HD, DB), BF),
        ),
        in_specs=[hb, hb, vm, vm, vm, sm, sm, vm, vm],
        out_specs=(vm, vm),
        scratch_shapes=[
            pltpu.VMEM((2 * TOK, D), BF),
            pltpu.VMEM((NZ, NYH, n, QW), BF),
            pltpu.VMEM((NZ * ROWS, D), BF),
            pltpu.VMEM((NZ * ROWS, D), BF),
            pltpu.VMEM((D, 3 * HD), BF),
            pltpu.VMEM((NZ * ROWS, 2 * HD), F32),
            pltpu.VMEM((NZ * ROWS, HD), F32),
            pltpu.VMEM((2 * HD, NZ * ROWS), BF),
            pltpu.VMEM((HD, NZ * ROWS), BF),
            pltpu.VMEM((NZ, Q * ROWS, QW), F32),
            pltpu.VMEM((NYH, CH, Q * SLOT, CW), BF),
            pltpu.VMEM((NYH, CH, Q * SLOT, CW), BF),
            pltpu.VMEM((2, 4, CH, Q * ROWS, CW), BF),
            pltpu.VMEM((2, 4, CH, Q * ROWS, CW), BF),
            pltpu.VMEM((NX, 2, 3 * HD, DB), F32),
            pltpu.VMEM((NX, 2, 3 * HD, DB), BF),
            pltpu.VMEM((NX, 2, 3 * HD, DB), BF),
            pltpu.VMEM((2, 6, WH, DB), BF),
            pltpu.VMEM((2, 6, WH, DB), BF),
            pltpu.VMEM((2, WH, DB), BF),
            pltpu.VMEM((2, WH, DB), BF),
            dma((2,)),
            dma((2, 4, NYH, 2)), dma((2, 4, NYH, 2)),
            dma((NYH, 2)), dma((NYH, 2)),
            dma((NZ, 2)), dma((NZ, 2)),
            dma((2,)),
            dma((2, 2, 2)), dma((2, 2, 2)),
            dma((8,)), dma((8,)),
            dma((2, 4, CH)), dma((2, 4, CH)),
            dma((NYH, CH)), dma((NYH, CH)),
            dma((NX,)), dma((NX,)),
            dma((2, 6)), dma((2, 6)),
            dma((2,)), dma((2,)),
        ],
        compiler_params=pltpu.CompilerParams(
            collective_id=0, has_side_effects=True, vmem_limit_bytes=56 * 2 ** 20
        ),
        cost_estimate=pl.CostEstimate(flops=2 * 10 ** 9, bytes_accessed=4 * 2 ** 20, transcendentals=0),
    )(
        tokens, grad_out, gate_w, up_w, down_w, take_count, picked,
        jnp.asarray(gather_perm(), BF), jnp.asarray(scatter_perm(), BF),
    )
    return pl.pallas_call(
        finish,
        out_shape=(
            jax.ShapeDtypeStruct((1, TOK, D), BF),
            jax.ShapeDtypeStruct((DB, HD), BF),
            jax.ShapeDtypeStruct((DB, HD), BF),
            jax.ShapeDtypeStruct((DB, HD), BF),
        ),
        in_specs=[sm, sm, vm, vm],
        out_specs=(vm, vm, vm, vm),
    )(take_count, picked, fin, wg)


def solution(mesh):
    rows = P("group", "expert", None)
    flat = P("group", "expert")
    return jax.shard_map(
        local,
        mesh=mesh,
        in_specs=(rows, rows, flat, flat, flat, flat, rows),
        out_specs=(rows, flat, flat, flat),
        check_vma=False,
    )
```

```python
import heapq

import jax
import jax.numpy as jnp
import numpy as np
from jax import lax
from jax.experimental import pallas as pl
from jax.experimental.pallas import tpu as pltpu
from jax.sharding import PartitionSpec as P

BF = jnp.bfloat16
F32 = jnp.float32
SLOT = 6
NX, NYH, NZ = 4, 4, 8
TOK = 128
D = 4096
HD = 128
DB = 256
Q = 8
QW = D // Q
ROWS = NYH * SLOT
CH = 4
CW = QW // CH
MESH = pl.DeviceIdType.MESH
POS = {0: 0, 1: 1, 7: 2, 2: 3, 6: 4, 3: 5, 5: 6, 4: 7}
RANK = {"permute": 0, "forward": 1, "rows": 2}
GROUPS = ((0,), (1, 7), (2, 6), (3, 5, 4))


def mod(a, n):
    return lax.rem(a + n, n)


def gather_perm():
    n = NYH * Q * 2 * SLOT
    m = np.zeros((n, n), np.float32)
    for u in range(NYH):
        for q in range(Q):
            for t in range(2):
                for s in range(SLOT):
                    m[((q * 2 + t) * NYH + u) * SLOT + s, ((u * Q + q) * 2 + t) * SLOT + s] = 1
    return m


def scatter_perm():
    n = NYH * Q * SLOT
    m = np.zeros((n, n), np.float32)
    for u in range(NYH):
        for q in range(Q):
            for s in range(SLOT):
                m[(u * Q + q) * SLOT + s, (q * NYH + u) * SLOT + s] = 1
    return m


def gather_plan():
    unit = 1.05
    free = {}
    heap = []
    order = []
    got = {}
    need = {zr: 8 for zr in range(NZ)}
    need[0] = 6
    weights_left = 17
    tasks = []
    done = set()

    def send(t, key, link, length, lat):
        start = max(t, free.get(link, 0.0))
        free[link] = start + length
        heapq.heappush(heap, (start + length + lat, len(order), key))
        order.append(("send", key))

    def z_send(t, k, u, h, sg):
        send(t, ("z", k, u, h, sg), ("z", sg), unit, 3.3)

    def far_send(t, zr, sg):
        send(t, ("f", zr, sg), ("y", sg), 2 * unit, 4.5)

    def passes(t, zr, u, h):
        if u == 1 and h == 0:
            far_send(t, zr, -1)
        if u == 3 and h == 1:
            far_send(t, zr, 1)

    def core_send(t, dx, st):
        send(t, ("wc", dx, st), "core", 0.7, 0.9)

    for h in (0, 1):
        for sg in (1, -1):
            send(0, ("y", (-sg) % NYH, h), ("y", sg), 2 * unit, 4.5)
        for sg in (1, -1):
            z_send(0, 1, 0, h, sg)
    for sg in (1, -1):
        send(0, ("w1", 0, sg), ("x", sg), 4.2, 2.9)
    core_send(0, 0, 0)
    send(0, ("wl",), ("y", 1), 4.2, 2.9)

    t = 0.0
    while heap or tasks:
        if heap and heap[0][0] <= t + 0.2 or not tasks:
            at, _, key = heapq.heappop(heap)
            t = max(t, at) + 0.1
            order.append(("wait", key))
            kind = key[0]
            zr = None
            if kind == "y":
                _, u, h = key
                zr = 0
                for sg in (1, -1):
                    z_send(t, 1, u, h, sg)
                passes(t, 0, u, h)
            elif kind == "z":
                _, k, u, h, sg = key
                zr = (-sg * k) % NZ
                if k < 3 or (k == 3 and h == (0 if sg > 0 else 1)):
                    z_send(t, k + 1, u, h, sg)
                passes(t, zr, u, h)
            elif kind == "f":
                zr = key[1]
            else:
                weights_left -= 1
                if kind == "wl":
                    for sg in (1, -1):
                        send(t, ("w1", 1, sg), ("x", sg), 4.2, 2.9)
                    core_send(t, 0, 1)
                elif kind == "w1":
                    _, st, sg = key
                    send(t, ("w2", st, sg), ("x", sg), 2.1, 2.9)
                    core_send(t, (-sg) % NX, st)
                elif kind == "w2":
                    got[key[:2]] = got.get(key[:2], 0) + 1
                    if got[key[:2]] == 2:
                        core_send(t, 2, key[1])
            if zr is not None:
                got[zr] = got.get(zr, 0) + 1
                if got[zr] == need[zr]:
                    tasks.append(("permute", zr))
        else:
            tasks.sort(key=lambda k: RANK[k[0]])
            if not heap and tasks[0][0] == "rows":
                break
            task = tasks.pop(0)
            order.append(task)
            t += 0.4 if task[0] == "permute" else 0.8
            done.add(task)
            if task[0] == "forward" and 4 not in task[1]:
                tasks.append(("rows", task[1]))
        for grp in GROUPS:
            if weights_left == 0 and ("forward", grp) not in done and ("forward", grp) not in tasks:
                if all(("permute", zr) in done for zr in grp):
                    tasks.append(("forward", grp))
    return order, [k[1] for k in tasks]


def kernel(
    tok_hbm, dy_hbm, gw_hbm, uw_hbm, dw_hbm, cnt_ref, row_ref, gp_hbm, sp_hbm,
    fin_ref, wg_ref,
    td, gp_ref, sp_ref, Z, RX, RD, W, J, H, JT, HT, PP, Y0, YR, ZS, ZR, SS, ES, ER, XS, XR, LS, LR,
    in_sem, zss, zrs, yss, yrs, fss, frs, wl, wxs, wxr, wcs, wcr, rzs, rzr, rys, ryr, ecs, ecr, xss, xrs, lss, lrs,
):
    g = lax.axis_index("group")
    e = lax.axis_index("expert")
    x, yl, c = g // 4, (g // 2) % 2, g % 2
    yh, z = e // NZ, e % NZ

    def at(dx=0, dyl=0, dc=0, dyh=0, dz=0):
        xx = mod(x + dx, NX)
        yy = 1 - yl if dyl else yl
        cc = 1 - c if dc else c
        return ((xx * 2 + yy) * 2 + cc, mod(yh + dyh, NYH) * NZ + mod(z + dz, NZ))

    def rc(src, dst, ss, rs, dev):
        return pltpu.make_async_remote_copy(src, dst, ss, rs, device_id=dev, device_id_type=MESH)

    sends = []

    def go(cp):
        cp.start()
        sends.append(cp)

    bar = pltpu.get_barrier_semaphore()
    peers = [at(dyh=1), at(dyh=2), at(dyh=3), at(dz=1), at(dz=-1), at(dx=1), at(dx=-1), at(dyl=1), at(dc=1)]
    for p in peers:
        pl.semaphore_signal(bar, inc=1, device_id=p, device_id_type=MESH)

    def wid(dx=0, dyl=0, dc=0):
        return at(dx=dx, dyl=dyl, dc=dc)[0]

    def wrows(i, lo=0, n=DB):
        return pl.ds(pl.multiple_of(i * DB + lo, n), n)

    cols = [slice(0, D // 2), slice(D // 2, D)]
    loads = [
        pltpu.make_async_copy(src.at[0, :, cols[h]], td.at[t * TOK:(t + 1) * TOK, cols[h]], in_sem.at[2 * h + t])
        for h in (0, 1) for t, src in enumerate((tok_hbm, dy_hbm))
    ]
    w_loads = [
        pltpu.make_async_copy(src, W.at[wrows(g), k * HD:(k + 1) * HD], in_sem.at[4 + k])
        for k, src in enumerate((gw_hbm, uw_hbm, dw_hbm))
    ]
    p_loads = [
        pltpu.make_async_copy(gp_hbm, gp_ref, in_sem.at[7]),
        pltpu.make_async_copy(sp_hbm, sp_ref, in_sem.at[8]),
    ]
    for cp in loads + w_loads + p_loads:
        cp.start()

    n = 2 * SLOT * Q
    HB = n // 2
    r_i = lax.broadcasted_iota(jnp.int32, (n, 2 * TOK), 0)
    k_i = lax.broadcasted_iota(jnp.int32, (n, 2 * TOK), 1)
    q_i = r_i // (2 * SLOT)
    ts = r_i - q_i * (2 * SLOT)
    want = jnp.full((n, 2 * TOK), -1, jnp.int32)
    cnt = cnt_ref[0, 0]
    for s in range(SLOT):
        p = jnp.where(s < cnt, row_ref[0, s], -TOK - 1)
        want = jnp.where(ts == s, p, want)
        want = jnp.where(ts == SLOT + s, p + TOK, want)
    hit = (want == k_i) & (want >= jnp.where(ts < SLOT, 0, TOK))
    def choose(h):
        loads[2 * h].wait()
        loads[2 * h + 1].wait()
        r0 = h * HB
        acc = jnp.zeros((HB, QW), F32)
        for q in range(h * Q // 2, (h + 1) * Q // 2):
            eq = jnp.where(hit[r0:r0 + HB] & (q_i[r0:r0 + HB] == q), 1.0, 0.0).astype(BF)
            acc = acc + jnp.dot(eq, td[:, q * QW:(q + 1) * QW], preferred_element_type=F32)
        Z[0, 0, r0:r0 + HB] = acc.astype(BF)

    choose(0)
    pl.semaphore_wait(bar, len(peers))

    def half(h):
        return slice(h * HB, (h + 1) * HB)

    def dirn(sg):
        return 0 if sg > 0 else 1

    cps = {}
    for sg in (1, -1):
        d = dirn(sg)
        for h in (0, 1):
            u = (-sg) % NYH
            cps["y", u, h] = rc(Z.at[0, 0, half(h)], Z.at[0, u, half(h)], yss.at[u, h], yrs.at[u, h], at(dyh=sg))
            for k in (1, 2, 3, 4):
                if k == 4 and h != d:
                    continue
                for u in (0, 1, 3):
                    src, dst = (-sg * (k - 1)) % NZ, (-sg * k) % NZ
                    cps["z", k, u, h, sg] = rc(
                        Z.at[src, u, half(h)], Z.at[dst, u, half(h)],
                        zss.at[d, k - 1, u, h], zrs.at[d, k - 1, u, h], at(dz=sg),
                    )
        for zr in range(NZ):
            u, h = (3, 1) if sg > 0 else (1, 0)
            cps["f", zr, sg] = rc(
                Z.at[zr, u, half(h)], Z.at[zr, 2, half(h)], fss.at[zr, d], frs.at[zr, d], at(dyh=sg)
            )
        for st in (0, 1):
            r = wrows(wid(dyl=st))
            cps["w1", st, sg] = rc(W.at[r], W.at[r], wxs.at[d, 0, st], wxr.at[d, 0, st], at(dx=sg))
            r = wrows(wid(dx=-sg, dyl=st), d * (DB // 2), DB // 2)
            cps["w2", st, sg] = rc(W.at[r], W.at[r], wxs.at[d, 1, st], wxr.at[d, 1, st], at(dx=sg))
    cps["wl",] = rc(W.at[wrows(g)], W.at[wrows(g)], wl.at[0], wl.at[1], at(dyl=1))
    for dx in range(NX):
        for st in (0, 1):
            r = wrows(wid(dx=dx, dyl=st))
            cps["wc", dx, st] = rc(W.at[r], W.at[r], wcs.at[dx * 2 + st], wcr.at[dx * 2 + st], at(dc=1))

    p_ready = []

    def permute(zr):
        if not p_ready:
            p_loads[0].wait()
            p_ready.append(True)
        src = Z[zr].reshape(NYH * n, QW)
        out = jnp.dot(gp_ref[...], src, preferred_element_type=F32).astype(BF)
        r0 = POS[zr] * ROWS
        for q in range(Q):
            RX[r0:r0 + ROWS, q * QW:(q + 1) * QW] = out[q * 48:q * 48 + 24]
            RD[r0:r0 + ROWS, q * QW:(q + 1) * QW] = out[q * 48 + 24:q * 48 + 48]

    def group_rows(grp):
        return slice(POS[grp[0]] * ROWS, (POS[grp[-1]] + 1) * ROWS)

    def forward(grp):
        r = group_rows(grp)
        pre = jnp.dot(RX[r], W[:, 0:2 * HD], preferred_element_type=F32)
        gh = jnp.dot(RD[r], W[:, 2 * HD:], preferred_element_type=F32)
        gate = pre[:, 0:HD]
        up = pre[:, HD:]
        sg = 1.0 / (1.0 + jnp.exp(-gate))
        act = gate * sg
        J[r, 0:HD] = gh * up * sg * (1.0 + gate * (1.0 - sg))
        J[r, HD:] = gh * act
        H[r] = act * up

    def row_grad(grp):
        j = J[group_rows(grp)].astype(BF)
        for q in range(Q):
            res = lax.dot_general(
                j, W[q * QW:(q + 1) * QW, 0:2 * HD], (((1,), (1,)), ((), ())), preferred_element_type=F32
            )
            for k, zr in enumerate(grp):
                PP[zr, q * ROWS:(q + 1) * ROWS, :] = res[k * ROWS:(k + 1) * ROWS]

    first = True
    steps, later = gather_plan()
    for step in steps:
        what, arg = step
        if first and (arg[0][0] == "w" or arg[-1 if arg[0] == "y" else 3] == 1):
            first = False
            choose(1)
            for cp in w_loads:
                cp.wait()
        if what == "send":
            go(cps[arg])
        elif what == "wait":
            cps[arg].wait_recv()
        elif what == "permute":
            permute(arg)
        elif what == "forward":
            forward(arg)
        else:
            row_grad(arg)

    for cp in p_loads[1:]:
        cp.wait()

    def lanes(cc):
        return slice(cc * CW, (cc + 1) * CW)

    far = {1: (0, 1), -1: (2, 3)}
    order = {1: (2, 3, 0, 1), -1: (0, 1, 2, 3)}
    rzc = {}
    for sg in (1, -1):
        d = dirn(sg)
        for k in (1, 2, 3, 4):
            for cc in (far[sg] if k == 1 else range(CH)):
                rzc[k, cc, sg] = rc(
                    ZS.at[d, k - 1, cc], ZR.at[d, k - 1, cc], rzs.at[d, k - 1, cc], rzr.at[d, k - 1, cc], at(dz=sg)
                )

    def rz_hop(k, part=range(CH)):
        for i in part:
            for sg in (1, -1):
                d = dirn(sg)
                zr = (sg * (5 - k)) % NZ
                if k == 1:
                    if i >= 2:
                        continue
                    cc = far[sg][i]
                    val = PP[zr, :, lanes(cc)]
                else:
                    cc = order[sg][i]
                    val = PP[zr, :, lanes(cc)]
                    if k > 2 or cc in far[sg]:
                        rzc[k - 1, cc, sg].wait_recv()
                        val = val + ZR[d, k - 2, cc].astype(F32)
                ZS[d, k - 1, cc] = val.astype(BF)
                go(rzc[k, cc, sg])

    row_grad((4,))
    rz_hop(1)
    row_grad((3, 5))
    rz_hop(2, (0, 1))
    for grp in reversed(later):
        row_grad(grp)

    JT[...] = J[...].T.astype(BF)
    HT[...] = H[...].T.astype(BF)
    ec = {dx: rc(ES.at[dx], ER.at[dx], ecs.at[dx], ecr.at[dx], at(dc=1)) for dx in range(NX)}

    def wgrad(dst, dx, st, dc):
        i = wid(dx=dx, dyl=st, dc=dc)
        ln = pl.ds(pl.multiple_of(i * DB, DB), DB)
        dst[dx, st, 0:2 * HD] = jnp.dot(JT[...], RX[:, ln], preferred_element_type=F32).astype(dst.dtype)
        dst[dx, st, 2 * HD:] = jnp.dot(HT[...], RD[:, ln], preferred_element_type=F32).astype(dst.dtype)

    def other_core(dx):
        for st in (0, 1):
            wgrad(ES, dx, st, 1)
        go(ec[dx])

    def own_core(dx):
        for st in (0, 1):
            wgrad(SS, dx, st, 0)

    WH = 3 * HD // 2
    xc = {}
    for sg in (1, -1):
        for it in range(6):
            d = dirn(sg)
            xc[sg, it] = rc(XS.at[d, it], XR.at[d, it], xss.at[d, it], xrs.at[d, it], at(dx=sg))

    def piece(sg, it):
        d = dirn(sg)
        st = (1, 0, 1, 1, 0, 0)[it]
        h = 1 - d if it in (2, 4) else d
        dx = 2 if it < 2 else sg % NX
        hs = slice(h * WH, (h + 1) * WH)
        val = SS[dx, st, hs] + ER[dx, st, hs].astype(F32)
        if it in (3, 5):
            prev = 0 if it == 3 else 1
            xc[sg, prev].wait_recv()
            val = val + XR[d, prev].astype(F32)
        XS[d, it] = val.astype(BF)
        go(xc[sg, it])

    def both_ways(it):
        piece(1, it)
        piece(-1, it)

    other_core(2)
    own_core(2)
    rz_hop(2, (2, 3))
    ec[2].wait_recv()
    both_ways(0)
    both_ways(1)
    other_core(1)
    other_core(3)
    rz_hop(3)
    own_core(1)
    own_core(3)
    ec[1].wait_recv()
    ec[3].wait_recv()
    both_ways(2)
    rz_hop(4)
    both_ways(3)
    both_ways(4)
    other_core(0)
    own_core(0)
    both_ways(5)

    ry = {
        (u, cc): rc(Y0.at[u, cc], YR.at[(-u) % NYH, cc], rys.at[u, cc], ryr.at[(-u) % NYH, cc], at(dyh=u))
        for u in (1, 2, 3) for cc in range(CH)
    }
    for cc in (2, 0, 3, 1):
        rzc[4, cc, 1].wait_recv()
        rzc[4, cc, -1].wait_recv()
        tot = PP[0, :, lanes(cc)] + ZR[0, 3, cc].astype(F32) + ZR[1, 3, cc].astype(F32)
        out = jnp.dot(sp_ref[...], tot.astype(BF), preferred_element_type=F32).astype(BF)
        for u in range(NYH):
            Y0[u, cc] = out[u * 48:(u + 1) * 48]
        for u in (2, 1, 3):
            go(ry[u, cc])

    ec[0].wait_recv()

    def x_total(st, h):
        hs = slice(h * WH, (h + 1) * WH)
        val = SS[0, st, hs] + ER[0, st, hs].astype(F32)
        for sg in (1, -1):
            d = dirn(sg)
            it = (2 if st else 4) + (1 if h == d else 0)
            xc[sg, it].wait_recv()
            val = val + XR[d, it].astype(F32)
        return val

    lc = [rc(LS.at[h], LR.at[h], lss.at[h], lrs.at[h], at(dyl=1)) for h in (0, 1)]
    for h in (0, 1):
        LS[h] = x_total(1, h).astype(BF)
        go(lc[h])
    for h in (0, 1):
        SS[1, 0, h * WH:(h + 1) * WH] = x_total(0, h)

    for cc in range(CH):
        for u in (1, 2, 3):
            ry[u, cc].wait_recv()
        fin_ref[:, lanes(cc)] = (
            Y0[0, cc].astype(F32) + YR[1, cc].astype(F32) + YR[2, cc].astype(F32) + YR[3, cc].astype(F32)
        ).astype(BF)
    for h in (0, 1):
        hs = slice(h * WH, (h + 1) * WH)
        lc[h].wait_recv()
        wg_ref[hs] = ((SS[1, 0, hs] + LR[h].astype(F32)) * (1.0 / 16.0)).astype(BF)

    for cp in sends:
        cp.wait_send()


def finish(cnt_ref, row_ref, fin_ref, wg_ref, gt_ref, gg_ref, gu_ref, gd_ref):
    cnt = cnt_ref[0, 0]
    o_t = lax.broadcasted_iota(jnp.int32, (TOK, Q * SLOT), 0)
    o_r = lax.broadcasted_iota(jnp.int32, (TOK, Q * SLOT), 1)
    o_q = o_r // SLOT
    o_s = o_r - o_q * SLOT
    row_of = jnp.full((TOK, Q * SLOT), -1, jnp.int32)
    for s in range(SLOT):
        row_of = jnp.where(o_s == s, jnp.where(s < cnt, row_ref[0, s], -1), row_of)
    place = row_of == o_t
    for q in range(Q):
        oh = jnp.where(place & (o_q == q), 1.0, 0.0).astype(BF)
        gt_ref[0, :, q * QW:(q + 1) * QW] = jnp.dot(oh, fin_ref[...], preferred_element_type=F32).astype(BF)
    for k, ref in enumerate((gg_ref, gu_ref, gd_ref)):
        ref[...] = wg_ref[k * HD:(k + 1) * HD].astype(F32).T.astype(BF)


def local(tokens, grad_out, gate_w, up_w, down_w, take_count, take_rows):
    vm = pl.BlockSpec(memory_space=pltpu.VMEM)
    sm = pl.BlockSpec(memory_space=pltpu.SMEM)
    hb = pl.BlockSpec(memory_space=pl.ANY)
    dma = pltpu.SemaphoreType.DMA
    n = 2 * SLOT * Q
    WH = 3 * HD // 2
    picked = take_rows.reshape(1, SLOT)
    fin, wg = pl.pallas_call(
        kernel,
        out_shape=(
            jax.ShapeDtypeStruct((Q * SLOT, QW), BF),
            jax.ShapeDtypeStruct((3 * HD, DB), BF),
        ),
        in_specs=[hb, hb, hb, hb, hb, sm, sm, hb, hb],
        out_specs=(vm, vm),
        scratch_shapes=[
            pltpu.VMEM((2 * TOK, D), BF),
            pltpu.VMEM((NYH * n, NYH * n), BF),
            pltpu.VMEM((NYH * n // 2, NYH * n // 2), BF),
            pltpu.VMEM((NZ, NYH, n, QW), BF),
            pltpu.VMEM((NZ * ROWS, D), BF),
            pltpu.VMEM((NZ * ROWS, D), BF),
            pltpu.VMEM((D, 3 * HD), BF),
            pltpu.VMEM((NZ * ROWS, 2 * HD), F32),
            pltpu.VMEM((NZ * ROWS, HD), F32),
            pltpu.VMEM((2 * HD, NZ * ROWS), BF),
            pltpu.VMEM((HD, NZ * ROWS), BF),
            pltpu.VMEM((NZ, Q * ROWS, QW), F32),
            pltpu.VMEM((NYH, CH, Q * SLOT, CW), BF),
            pltpu.VMEM((NYH, CH, Q * SLOT, CW), BF),
            pltpu.VMEM((2, 4, CH, Q * ROWS, CW), BF),
            pltpu.VMEM((2, 4, CH, Q * ROWS, CW), BF),
            pltpu.VMEM((NX, 2, 3 * HD, DB), F32),
            pltpu.VMEM((NX, 2, 3 * HD, DB), BF),
            pltpu.VMEM((NX, 2, 3 * HD, DB), BF),
            pltpu.VMEM((2, 6, WH, DB), BF),
            pltpu.VMEM((2, 6, WH, DB), BF),
            pltpu.VMEM((2, WH, DB), BF),
            pltpu.VMEM((2, WH, DB), BF),
            dma((9,)),
            dma((2, 4, NYH, 2)), dma((2, 4, NYH, 2)),
            dma((NYH, 2)), dma((NYH, 2)),
            dma((NZ, 2)), dma((NZ, 2)),
            dma((2,)),
            dma((2, 2, 2)), dma((2, 2, 2)),
            dma((8,)), dma((8,)),
            dma((2, 4, CH)), dma((2, 4, CH)),
            dma((NYH, CH)), dma((NYH, CH)),
            dma((NX,)), dma((NX,)),
            dma((2, 6)), dma((2, 6)),
            dma((2,)), dma((2,)),
        ],
        compiler_params=pltpu.CompilerParams(
            collective_id=0, has_side_effects=True, vmem_limit_bytes=56 * 2 ** 20
        ),
        cost_estimate=pl.CostEstimate(flops=2 * 10 ** 9, bytes_accessed=4 * 2 ** 20, transcendentals=0),
    )(
        tokens, grad_out, gate_w, up_w, down_w, take_count, picked,
        jnp.asarray(gather_perm(), BF), jnp.asarray(scatter_perm(), BF),
    )
    return pl.pallas_call(
        finish,
        out_shape=(
            jax.ShapeDtypeStruct((1, TOK, D), BF),
            jax.ShapeDtypeStruct((DB, HD), BF),
            jax.ShapeDtypeStruct((DB, HD), BF),
            jax.ShapeDtypeStruct((DB, HD), BF),
        ),
        in_specs=[sm, sm, vm, vm],
        out_specs=(vm, vm, vm, vm),
    )(take_count, picked, fin, wg)


def solution(mesh):
    rows = P("group", "expert", None)
    flat = P("group", "expert")
    return jax.shard_map(
        local,
        mesh=mesh,
        in_specs=(rows, rows, flat, flat, flat, flat, rows),
        out_specs=(rows, flat, flat, flat),
        check_vma=False,
    )
```

```python
import heapq

import jax
import jax.numpy as jnp
import numpy as np
from jax import lax
from jax.experimental import pallas as pl
from jax.experimental.pallas import tpu as pltpu
from jax.sharding import PartitionSpec as P

BF = jnp.bfloat16
F32 = jnp.float32
SLOT = 6
NX, NYH, NZ = 4, 4, 8
TOK = 128
D = 4096
HD = 128
DB = 256
Q = 8
QW = D // Q
ROWS = NYH * SLOT
CH = 4
CW = QW // CH
MESH = pl.DeviceIdType.MESH
POS = {0: 0, 1: 1, 7: 2, 2: 3, 6: 4, 3: 5, 5: 6, 4: 7}
RANK = {"permute": 0, "forward": 1, "rows": 2}
GROUPS = ((0,), (1, 7), (2, 6), (3, 5, 4))


def mod(a, n):
    return lax.rem(a + n, n)


def gather_perm():
    n = NYH * Q * 2 * SLOT
    m = np.zeros((n, n), np.float32)
    for u in range(NYH):
        for q in range(Q):
            for t in range(2):
                for s in range(SLOT):
                    m[((q * 2 + t) * NYH + u) * SLOT + s, ((u * Q + q) * 2 + t) * SLOT + s] = 1
    return m


def scatter_perm():
    n = NYH * Q * SLOT
    m = np.zeros((n, n), np.float32)
    for u in range(NYH):
        for q in range(Q):
            for s in range(SLOT):
                m[(u * Q + q) * SLOT + s, (q * NYH + u) * SLOT + s] = 1
    return m


def gather_plan():
    unit = 1.05
    free = {}
    heap = []
    order = []
    got = {}
    need = {zr: 8 for zr in range(NZ)}
    need[0] = 6
    weights_left = 17
    tasks = []
    done = set()

    def send(t, key, link, length, lat):
        start = max(t, free.get(link, 0.0))
        free[link] = start + length
        heapq.heappush(heap, (start + length + lat, len(order), key))
        order.append(("send", key))

    def z_send(t, k, u, h, sg):
        send(t, ("z", k, u, h, sg), ("z", sg), unit, 3.3)

    def far_send(t, zr, sg):
        send(t, ("f", zr, sg), ("y", sg), 2 * unit, 4.5)

    def passes(t, zr, u, h):
        if u == 1 and h == 0:
            far_send(t, zr, -1)
        if u == 3 and h == 1:
            far_send(t, zr, 1)

    def core_send(t, dx, st):
        send(t, ("wc", dx, st), "core", 0.7, 0.9)

    for h in (0, 1):
        for sg in (1, -1):
            send(0, ("y", (-sg) % NYH, h), ("y", sg), 2 * unit, 4.5)
        for sg in (1, -1):
            z_send(0, 1, 0, h, sg)
    for sg in (1, -1):
        send(0, ("w1", 0, sg), ("x", sg), 4.2, 2.9)
    core_send(0, 0, 0)
    send(0, ("wl",), ("y", 1), 4.2, 2.9)

    t = 0.0
    while heap or tasks:
        if heap and heap[0][0] <= t + 0.2 or not tasks:
            at, _, key = heapq.heappop(heap)
            t = max(t, at) + 0.1
            order.append(("wait", key))
            kind = key[0]
            zr = None
            if kind == "y":
                _, u, h = key
                zr = 0
                for sg in (1, -1):
                    z_send(t, 1, u, h, sg)
                passes(t, 0, u, h)
            elif kind == "z":
                _, k, u, h, sg = key
                zr = (-sg * k) % NZ
                if k < 3 or (k == 3 and h == (0 if sg > 0 else 1)):
                    z_send(t, k + 1, u, h, sg)
                passes(t, zr, u, h)
            elif kind == "f":
                zr = key[1]
            else:
                weights_left -= 1
                if kind == "wl":
                    for sg in (1, -1):
                        send(t, ("w1", 1, sg), ("x", sg), 4.2, 2.9)
                    core_send(t, 0, 1)
                elif kind == "w1":
                    _, st, sg = key
                    send(t, ("w2", st, sg), ("x", sg), 2.1, 2.9)
                    core_send(t, (-sg) % NX, st)
                elif kind == "w2":
                    got[key[:2]] = got.get(key[:2], 0) + 1
                    if got[key[:2]] == 2:
                        core_send(t, 2, key[1])
            if zr is not None:
                got[zr] = got.get(zr, 0) + 1
                if got[zr] == need[zr]:
                    tasks.append(("permute", zr))
        else:
            tasks.sort(key=lambda k: RANK[k[0]])
            if not heap and tasks[0][0] == "rows":
                break
            task = tasks.pop(0)
            order.append(task)
            t += 0.4 if task[0] == "permute" else 0.8
            done.add(task)
            if task[0] == "forward" and 4 not in task[1]:
                tasks.append(("rows", task[1]))
        for grp in GROUPS:
            if weights_left == 0 and ("forward", grp) not in done and ("forward", grp) not in tasks:
                if all(("permute", zr) in done for zr in grp):
                    tasks.append(("forward", grp))
    return order, [k[1] for k in tasks]


def kernel(
    tok_hbm, dy_hbm, gw_hbm, uw_hbm, dw_hbm, cnt_ref, row_ref, gp_hbm, sp_hbm,
    fin_ref, wg_ref,
    td, gp_ref, sp_ref, Z, RX, RD, W, J, H, JT, HT, PP, Y0, YR, ZS, ZR, SS, ES, ER, XS, XR, LS, LR,
    in_sem, zss, zrs, yss, yrs, fss, frs, wl, wxs, wxr, wcs, wcr, rzs, rzr, rys, ryr, ecs, ecr, xss, xrs, lss, lrs,
):
    g = lax.axis_index("group")
    e = lax.axis_index("expert")
    x, yl, c = g // 4, (g // 2) % 2, g % 2
    yh, z = e // NZ, e % NZ

    def at(dx=0, dyl=0, dc=0, dyh=0, dz=0):
        xx = mod(x + dx, NX)
        yy = 1 - yl if dyl else yl
        cc = 1 - c if dc else c
        return ((xx * 2 + yy) * 2 + cc, mod(yh + dyh, NYH) * NZ + mod(z + dz, NZ))

    def rc(src, dst, ss, rs, dev):
        return pltpu.make_async_remote_copy(src, dst, ss, rs, device_id=dev, device_id_type=MESH)

    sends = []

    def go(cp):
        cp.start()
        sends.append(cp)

    bar = pltpu.get_barrier_semaphore()
    peers = [at(dyh=1), at(dyh=2), at(dyh=3), at(dz=1), at(dz=-1), at(dx=1), at(dx=-1), at(dyl=1), at(dc=1)]
    for p in peers:
        pl.semaphore_signal(bar, inc=1, device_id=p, device_id_type=MESH)

    def wid(dx=0, dyl=0, dc=0):
        return at(dx=dx, dyl=dyl, dc=dc)[0]

    def wrows(i, lo=0, n=DB):
        return pl.ds(pl.multiple_of(i * DB + lo, n), n)

    cols = [slice(0, D // 2), slice(D // 2, D)]
    loads = [
        pltpu.make_async_copy(src.at[0, :, cols[h]], td.at[t * TOK:(t + 1) * TOK, cols[h]], in_sem.at[2 * h + t])
        for h in (0, 1) for t, src in enumerate((tok_hbm, dy_hbm))
    ]
    w_loads = [
        pltpu.make_async_copy(src, W.at[wrows(g), k * HD:(k + 1) * HD], in_sem.at[4 + k])
        for k, src in enumerate((gw_hbm, uw_hbm, dw_hbm))
    ]
    p_loads = [
        pltpu.make_async_copy(gp_hbm, gp_ref, in_sem.at[7]),
        pltpu.make_async_copy(sp_hbm, sp_ref, in_sem.at[8]),
    ]
    for cp in loads + w_loads + p_loads:
        cp.start()

    n = 2 * SLOT * Q
    HB = n // 2
    r_i = lax.broadcasted_iota(jnp.int32, (n, 2 * TOK), 0)
    k_i = lax.broadcasted_iota(jnp.int32, (n, 2 * TOK), 1)
    q_i = r_i // (2 * SLOT)
    ts = r_i - q_i * (2 * SLOT)
    want = jnp.full((n, 2 * TOK), -1, jnp.int32)
    cnt = cnt_ref[0, 0]
    for s in range(SLOT):
        p = jnp.where(s < cnt, row_ref[0, s], -TOK - 1)
        want = jnp.where(ts == s, p, want)
        want = jnp.where(ts == SLOT + s, p + TOK, want)
    hit = (want == k_i) & (want >= jnp.where(ts < SLOT, 0, TOK))
    def choose(h):
        loads[2 * h].wait()
        loads[2 * h + 1].wait()
        r0 = h * HB
        acc = jnp.zeros((HB, QW), F32)
        for q in range(h * Q // 2, (h + 1) * Q // 2):
            eq = jnp.where(hit[r0:r0 + HB] & (q_i[r0:r0 + HB] == q), 1.0, 0.0).astype(BF)
            acc = acc + jnp.dot(eq, td[:, q * QW:(q + 1) * QW], preferred_element_type=F32)
        Z[0, 0, r0:r0 + HB] = acc.astype(BF)

    choose(0)
    pl.semaphore_wait(bar, len(peers))

    def half(h):
        return slice(h * HB, (h + 1) * HB)

    def dirn(sg):
        return 0 if sg > 0 else 1

    cps = {}
    for sg in (1, -1):
        d = dirn(sg)
        for h in (0, 1):
            u = (-sg) % NYH
            cps["y", u, h] = rc(Z.at[0, 0, half(h)], Z.at[0, u, half(h)], yss.at[u, h], yrs.at[u, h], at(dyh=sg))
            for k in (1, 2, 3, 4):
                if k == 4 and h != d:
                    continue
                for u in (0, 1, 3):
                    src, dst = (-sg * (k - 1)) % NZ, (-sg * k) % NZ
                    cps["z", k, u, h, sg] = rc(
                        Z.at[src, u, half(h)], Z.at[dst, u, half(h)],
                        zss.at[d, k - 1, u, h], zrs.at[d, k - 1, u, h], at(dz=sg),
                    )
        for zr in range(NZ):
            u, h = (3, 1) if sg > 0 else (1, 0)
            cps["f", zr, sg] = rc(
                Z.at[zr, u, half(h)], Z.at[zr, 2, half(h)], fss.at[zr, d], frs.at[zr, d], at(dyh=sg)
            )
        for st in (0, 1):
            r = wrows(wid(dyl=st))
            cps["w1", st, sg] = rc(W.at[r], W.at[r], wxs.at[d, 0, st], wxr.at[d, 0, st], at(dx=sg))
            r = wrows(wid(dx=-sg, dyl=st), d * (DB // 2), DB // 2)
            cps["w2", st, sg] = rc(W.at[r], W.at[r], wxs.at[d, 1, st], wxr.at[d, 1, st], at(dx=sg))
    cps["wl",] = rc(W.at[wrows(g)], W.at[wrows(g)], wl.at[0], wl.at[1], at(dyl=1))
    for dx in range(NX):
        for st in (0, 1):
            r = wrows(wid(dx=dx, dyl=st))
            cps["wc", dx, st] = rc(W.at[r], W.at[r], wcs.at[dx * 2 + st], wcr.at[dx * 2 + st], at(dc=1))

    p_ready = []

    def permute(zr):
        if not p_ready:
            p_loads[0].wait()
            p_ready.append(True)
        src = Z[zr].reshape(NYH * n, QW)
        out = jnp.dot(gp_ref[...], src, preferred_element_type=F32).astype(BF)
        r0 = POS[zr] * ROWS
        for q in range(Q):
            RX[r0:r0 + ROWS, q * QW:(q + 1) * QW] = out[q * 48:q * 48 + 24]
            RD[r0:r0 + ROWS, q * QW:(q + 1) * QW] = out[q * 48 + 24:q * 48 + 48]

    def group_rows(grp):
        return slice(POS[grp[0]] * ROWS, (POS[grp[-1]] + 1) * ROWS)

    def forward(grp):
        r = group_rows(grp)
        pre = jnp.dot(RX[r], W[:, 0:2 * HD], preferred_element_type=F32)
        gh = jnp.dot(RD[r], W[:, 2 * HD:], preferred_element_type=F32)
        gate = pre[:, 0:HD]
        up = pre[:, HD:]
        sg = 1.0 / (1.0 + jnp.exp(-gate))
        act = gate * sg
        J[r, 0:HD] = gh * up * sg * (1.0 + gate * (1.0 - sg))
        J[r, HD:] = gh * act
        H[r] = act * up

    def row_grad(grp):
        j = J[group_rows(grp)].astype(BF)
        for q in range(Q):
            res = lax.dot_general(
                j, W[q * QW:(q + 1) * QW, 0:2 * HD], (((1,), (1,)), ((), ())), preferred_element_type=F32
            )
            for k, zr in enumerate(grp):
                PP[zr, q * ROWS:(q + 1) * ROWS, :] = res[k * ROWS:(k + 1) * ROWS]

    first = True
    steps, later = gather_plan()
    for step in steps:
        what, arg = step
        if first and (arg[0][0] == "w" or arg[-1 if arg[0] == "y" else 3] == 1):
            first = False
            choose(1)
            for cp in w_loads:
                cp.wait()
        if what == "send":
            go(cps[arg])
        elif what == "wait":
            cps[arg].wait_recv()
        elif what == "permute":
            permute(arg)
        elif what == "forward":
            forward(arg)
        else:
            row_grad(arg)

    for cp in p_loads[1:]:
        cp.wait()

    def lanes(cc):
        return slice(cc * CW, (cc + 1) * CW)

    far = {1: (0, 1), -1: (2, 3)}
    order = {1: (2, 3, 0, 1), -1: (0, 1, 2, 3)}
    rzc = {}
    for sg in (1, -1):
        d = dirn(sg)
        for k in (1, 2, 3, 4):
            for cc in (far[sg] if k == 1 else range(CH)):
                rzc[k, cc, sg] = rc(
                    ZS.at[d, k - 1, cc], ZR.at[d, k - 1, cc], rzs.at[d, k - 1, cc], rzr.at[d, k - 1, cc], at(dz=sg)
                )

    def rz_hop(k, part=range(CH)):
        for i in part:
            for sg in (1, -1):
                d = dirn(sg)
                zr = (sg * (5 - k)) % NZ
                if k == 1:
                    if i >= 2:
                        continue
                    cc = far[sg][i]
                    val = PP[zr, :, lanes(cc)]
                else:
                    cc = order[sg][i]
                    val = PP[zr, :, lanes(cc)]
                    if k > 2 or cc in far[sg]:
                        rzc[k - 1, cc, sg].wait_recv()
                        val = val + ZR[d, k - 2, cc].astype(F32)
                ZS[d, k - 1, cc] = val.astype(BF)
                go(rzc[k, cc, sg])

    row_grad((4,))
    rz_hop(1)
    row_grad((3, 5))
    rz_hop(2, (0, 1))
    for grp in reversed(later):
        row_grad(grp)

    JT[...] = J[...].T.astype(BF)
    HT[...] = H[...].T.astype(BF)
    ec = {dx: rc(ES.at[dx], ER.at[dx], ecs.at[dx], ecr.at[dx], at(dc=1)) for dx in range(NX)}

    def wgrad(dst, dx, st, dc):
        i = wid(dx=dx, dyl=st, dc=dc)
        ln = pl.ds(pl.multiple_of(i * DB, DB), DB)
        dst[dx, st, 0:2 * HD] = jnp.dot(JT[...], RX[:, ln], preferred_element_type=F32).astype(dst.dtype)
        dst[dx, st, 2 * HD:] = jnp.dot(HT[...], RD[:, ln], preferred_element_type=F32).astype(dst.dtype)

    def other_core(dx):
        for st in (0, 1):
            wgrad(ES, dx, st, 1)
        go(ec[dx])

    def own_core(dx):
        for st in (0, 1):
            wgrad(SS, dx, st, 0)

    WH = 3 * HD // 2
    xc = {}
    for sg in (1, -1):
        for it in range(6):
            d = dirn(sg)
            xc[sg, it] = rc(XS.at[d, it], XR.at[d, it], xss.at[d, it], xrs.at[d, it], at(dx=sg))

    def piece(sg, it):
        d = dirn(sg)
        st = (1, 0, 1, 1, 0, 0)[it]
        h = 1 - d if it in (2, 4) else d
        dx = 2 if it < 2 else sg % NX
        hs = slice(h * WH, (h + 1) * WH)
        val = SS[dx, st, hs] + ER[dx, st, hs].astype(F32)
        if it in (3, 5):
            prev = 0 if it == 3 else 1
            xc[sg, prev].wait_recv()
            val = val + XR[d, prev].astype(F32)
        XS[d, it] = val.astype(BF)
        go(xc[sg, it])

    def both_ways(it):
        piece(1, it)
        piece(-1, it)

    other_core(2)
    own_core(2)
    rz_hop(2, (2, 3))
    ec[2].wait_recv()
    both_ways(0)
    both_ways(1)
    other_core(1)
    other_core(3)
    rz_hop(3)
    own_core(1)
    own_core(3)
    ec[1].wait_recv()
    ec[3].wait_recv()
    both_ways(2)
    rz_hop(4)
    both_ways(3)
    both_ways(4)
    other_core(0)
    own_core(0)
    both_ways(5)

    ec[0].wait_recv()

    def x_total(st, h):
        hs = slice(h * WH, (h + 1) * WH)
        val = SS[0, st, hs] + ER[0, st, hs].astype(F32)
        for sg in (1, -1):
            d = dirn(sg)
            it = (2 if st else 4) + (1 if h == d else 0)
            xc[sg, it].wait_recv()
            val = val + XR[d, it].astype(F32)
        return val

    lc = [rc(LS.at[h], LR.at[h], lss.at[h], lrs.at[h], at(dyl=1)) for h in (0, 1)]
    for h in (0, 1):
        LS[h] = x_total(1, h).astype(BF)
        go(lc[h])

    ry = {
        (u, cc): rc(Y0.at[u, cc], YR.at[(-u) % NYH, cc], rys.at[u, cc], ryr.at[(-u) % NYH, cc], at(dyh=u))
        for u in (1, 2, 3) for cc in range(CH)
    }
    for cc in (2, 0, 3, 1):
        rzc[4, cc, 1].wait_recv()
        rzc[4, cc, -1].wait_recv()
        tot = PP[0, :, lanes(cc)] + ZR[0, 3, cc].astype(F32) + ZR[1, 3, cc].astype(F32)
        out = jnp.dot(sp_ref[...], tot.astype(BF), preferred_element_type=F32).astype(BF)
        for u in range(NYH):
            Y0[u, cc] = out[u * 48:(u + 1) * 48]
        for u in (2, 1, 3):
            go(ry[u, cc])

    for h in (0, 1):
        SS[1, 0, h * WH:(h + 1) * WH] = x_total(0, h)

    for cc in range(CH):
        for u in (1, 2, 3):
            ry[u, cc].wait_recv()
        fin_ref[:, lanes(cc)] = (
            Y0[0, cc].astype(F32) + YR[1, cc].astype(F32) + YR[2, cc].astype(F32) + YR[3, cc].astype(F32)
        ).astype(BF)
    for h in (0, 1):
        hs = slice(h * WH, (h + 1) * WH)
        lc[h].wait_recv()
        wg_ref[hs] = ((SS[1, 0, hs] + LR[h].astype(F32)) * (1.0 / 16.0)).astype(BF)

    for cp in sends:
        cp.wait_send()


def finish(cnt_ref, row_ref, fin_ref, wg_ref, gt_ref, gg_ref, gu_ref, gd_ref):
    cnt = cnt_ref[0, 0]
    o_t = lax.broadcasted_iota(jnp.int32, (TOK, Q * SLOT), 0)
    o_r = lax.broadcasted_iota(jnp.int32, (TOK, Q * SLOT), 1)
    o_q = o_r // SLOT
    o_s = o_r - o_q * SLOT
    row_of = jnp.full((TOK, Q * SLOT), -1, jnp.int32)
    for s in range(SLOT):
        row_of = jnp.where(o_s == s, jnp.where(s < cnt, row_ref[0, s], -1), row_of)
    place = row_of == o_t
    for q in range(Q):
        oh = jnp.where(place & (o_q == q), 1.0, 0.0).astype(BF)
        gt_ref[0, :, q * QW:(q + 1) * QW] = jnp.dot(oh, fin_ref[...], preferred_element_type=F32).astype(BF)
    for k, ref in enumerate((gg_ref, gu_ref, gd_ref)):
        ref[...] = wg_ref[k * HD:(k + 1) * HD].astype(F32).T.astype(BF)


def local(tokens, grad_out, gate_w, up_w, down_w, take_count, take_rows):
    vm = pl.BlockSpec(memory_space=pltpu.VMEM)
    sm = pl.BlockSpec(memory_space=pltpu.SMEM)
    hb = pl.BlockSpec(memory_space=pl.ANY)
    dma = pltpu.SemaphoreType.DMA
    n = 2 * SLOT * Q
    WH = 3 * HD // 2
    picked = take_rows.reshape(1, SLOT)
    fin, wg = pl.pallas_call(
        kernel,
        out_shape=(
            jax.ShapeDtypeStruct((Q * SLOT, QW), BF),
            jax.ShapeDtypeStruct((3 * HD, DB), BF),
        ),
        in_specs=[hb, hb, hb, hb, hb, sm, sm, hb, hb],
        out_specs=(vm, vm),
        scratch_shapes=[
            pltpu.VMEM((2 * TOK, D), BF),
            pltpu.VMEM((NYH * n, NYH * n), BF),
            pltpu.VMEM((NYH * n // 2, NYH * n // 2), BF),
            pltpu.VMEM((NZ, NYH, n, QW), BF),
            pltpu.VMEM((NZ * ROWS, D), BF),
            pltpu.VMEM((NZ * ROWS, D), BF),
            pltpu.VMEM((D, 3 * HD), BF),
            pltpu.VMEM((NZ * ROWS, 2 * HD), F32),
            pltpu.VMEM((NZ * ROWS, HD), F32),
            pltpu.VMEM((2 * HD, NZ * ROWS), BF),
            pltpu.VMEM((HD, NZ * ROWS), BF),
            pltpu.VMEM((NZ, Q * ROWS, QW), F32),
            pltpu.VMEM((NYH, CH, Q * SLOT, CW), BF),
            pltpu.VMEM((NYH, CH, Q * SLOT, CW), BF),
            pltpu.VMEM((2, 4, CH, Q * ROWS, CW), BF),
            pltpu.VMEM((2, 4, CH, Q * ROWS, CW), BF),
            pltpu.VMEM((NX, 2, 3 * HD, DB), F32),
            pltpu.VMEM((NX, 2, 3 * HD, DB), BF),
            pltpu.VMEM((NX, 2, 3 * HD, DB), BF),
            pltpu.VMEM((2, 6, WH, DB), BF),
            pltpu.VMEM((2, 6, WH, DB), BF),
            pltpu.VMEM((2, WH, DB), BF),
            pltpu.VMEM((2, WH, DB), BF),
            dma((9,)),
            dma((2, 4, NYH, 2)), dma((2, 4, NYH, 2)),
            dma((NYH, 2)), dma((NYH, 2)),
            dma((NZ, 2)), dma((NZ, 2)),
            dma((2,)),
            dma((2, 2, 2)), dma((2, 2, 2)),
            dma((8,)), dma((8,)),
            dma((2, 4, CH)), dma((2, 4, CH)),
            dma((NYH, CH)), dma((NYH, CH)),
            dma((NX,)), dma((NX,)),
            dma((2, 6)), dma((2, 6)),
            dma((2,)), dma((2,)),
        ],
        compiler_params=pltpu.CompilerParams(
            collective_id=0, has_side_effects=True, vmem_limit_bytes=56 * 2 ** 20
        ),
        cost_estimate=pl.CostEstimate(flops=2 * 10 ** 9, bytes_accessed=4 * 2 ** 20, transcendentals=0),
    )(
        tokens, grad_out, gate_w, up_w, down_w, take_count, picked,
        jnp.asarray(gather_perm(), BF), jnp.asarray(scatter_perm(), BF),
    )
    return pl.pallas_call(
        finish,
        out_shape=(
            jax.ShapeDtypeStruct((1, TOK, D), BF),
            jax.ShapeDtypeStruct((DB, HD), BF),
            jax.ShapeDtypeStruct((DB, HD), BF),
            jax.ShapeDtypeStruct((DB, HD), BF),
        ),
        in_specs=[sm, sm, vm, vm],
        out_specs=(vm, vm, vm, vm),
    )(take_count, picked, fin, wg)


def solution(mesh):
    rows = P("group", "expert", None)
    flat = P("group", "expert")
    return jax.shard_map(
        local,
        mesh=mesh,
        in_specs=(rows, rows, flat, flat, flat, flat, rows),
        out_specs=(rows, flat, flat, flat),
        check_vma=False,
    )
```
